256 devices in a mesh: band: 16 (over z, y_hi), fft: 16 (over y_lo, x, core).
Axes of the slice: x: 4, y: 4 (y_hi: 2, y_lo: 2; y = y_hi * 2 + y_lo), z: 8, core: 2. Of those that a mesh axis runs over, the one named last changes fastest.
Arguments:
- orbitals: float32 [32, 128, 128, 128], P('band', 'fft'), may hold values from -6 to 6
Outputs:
- applied: float32 [32, 128, 128, 128], P('band', 'fft')
- owner_terms: float32 [4, 128, 128, 128], P(None, 'fft')
The draws below stay inside these ranges and needn't reach their ends.
All inputs are finite; a program needn't handle non-finite values.
Results may differ from the reference program's by a relative error of at most 0.0001.
Values sent between devices are 32-bit elements; how exact they have to be, the bound alone decides.
No kernel may reach another device: no remote copies, remote signals or barrier semaphores. Data moves between devices by JAX's collectives and lax.ppermute only.
A program may use at most 128 MiB of HBM per device.

```python
import math
import jax
import jax.numpy as jnp
from jax import lax

NX = 128
NY = 128
NZ = 128
NB_DEV = 2
OWN = 2
STEPS = 2
BANDS = 32
N_BAND = 16


def block_scale(stream_key, shape, split, low, high):
    level, own = 1.0, jax.random.fold_in(stream_key, 6)
    for position, blocks in split:
        steps = jnp.exp(jax.random.uniform(jax.random.fold_in(own, position), (blocks,), jnp.float32, low / len(split), high / len(split)))
        level = level * jnp.repeat(steps, shape[position] // blocks).reshape([-1 if axis == position else 1 for axis in range(len(shape))])
    return level


def bell_draw(own_key, dims, deviation, most, pieces=(), kind=jnp.bfloat16):
    drawn = deviation * jax.random.normal(own_key, dims, jnp.float32)
    if pieces:
        drawn = drawn * block_scale(own_key, dims, pieces, -0.22, 0.18)
    return jnp.clip(drawn, -most, most).astype(kind)


def setup_inputs(seed: int = 0) -> dict:
    arg_keys = jax.random.split(jax.random.key(seed), 2)
    orbitals = bell_draw(arg_keys[0], (BANDS, NZ, NY, NX), 1.0, 6.0, ((0, 16), (1, 16)), jnp.float32)
    return {"orbitals": orbitals}


SPACING = 0.29
OMEGA = 0.106
MIX = -0.25


def wavenumber(n):
    idx = jnp.arange(n, dtype=jnp.int32)
    shifted = jnp.where(idx < n // 2, idx, idx - n)
    return (2.0 * math.pi / (n * SPACING)) * shifted.astype(jnp.float32)


def screened_kernel(nz, ny, nx):
    gz = wavenumber(nz)[:, None, None]
    gy = wavenumber(ny)[None, :, None]
    gx = wavenumber(nx)[None, None, :]
    ratio = (gz * gz + gy * gy + gx * gx) / (4.0 * OMEGA * OMEGA)
    safe = jnp.where(ratio > 0, ratio, 1.0)
    return (math.pi / (OMEGA * OMEGA)) * jnp.where(ratio > 0, -jnp.expm1(-safe) / safe, 1.0)


def reference(orbitals):
    kernel = screened_kernel(NZ, NY, NX)
    applied = jnp.zeros_like(orbitals)
    owner_list = []
    for step in range(STEPS):
        owner = (step * N_BAND) // STEPS
        for item in range(OWN):
            phi = orbitals[owner * NB_DEV + item]

            def pair(carry, orbit):
                density = phi * orbit
                potential = jnp.real(jnp.fft.ifftn(kernel * jnp.fft.fftn(density))).astype(orbitals.dtype)
                return carry + potential * orbit, potential * phi

            total, contrib = lax.scan(pair, jnp.zeros_like(phi), orbitals)
            applied = applied + MIX * contrib
            owner_list.append(MIX * total)
    return applied, jnp.stack(owner_list, 0)
```

```python
import math

import jax
import jax.numpy as jnp
import ml_dtypes
import numpy as np
from jax import lax
from jax.experimental import pallas as pl
from jax.experimental.pallas import tpu as pltpu
from jax.sharding import PartitionSpec as P

N = 128
SPACING = 0.29
OMEGA = 0.106
MIX = -0.25
VMEM = 48 * 1024 * 1024


def cas_tables():
    idx = np.arange(N)
    angle = 2.0 * np.pi / N * (idx[:, None] * idx[None, :] % N)
    full = np.cos(angle) + np.sin(angle)
    high = full.astype(ml_dtypes.bfloat16)
    low = (full - high.astype(np.float64)).astype(ml_dtypes.bfloat16)
    left = np.concatenate([high, low], 1)
    right = np.concatenate([left, left], 0)
    return left, right


def halves(value):
    high = value.astype(jnp.bfloat16)
    low = (value - high.astype(jnp.float32)).astype(jnp.bfloat16)
    return high, low


def dot(a, b):
    return lax.dot_general(a, b, (((1,), (0,)), ((), ())), preferred_element_type=jnp.float32)


def rows_by_table(value, right):
    out = dot(jnp.concatenate(halves(value), 1), right)
    return out[:, :N] + out[:, N:]


def table_by_rows(left, value):
    pair = jnp.concatenate(halves(value), 1)
    out = dot(left, jnp.concatenate([pair, pair], 0))
    size = value.shape[1]
    return out[:, :size] + out[:, size:]


def spread_kernel(phi_ref, orb_ref, left_ref, right_ref, out_ref):
    slab = orb_ref.shape[1]
    density = (phi_ref[0] * orb_ref[0]).reshape(slab * N, N)
    lines = rows_by_table(density, right_ref[...])
    flat = out_ref.reshape(N * slab, N)
    for z in range(slab):
        plane = table_by_rows(left_ref[...], lines[z * N:(z + 1) * N])
        flat[pl.ds(z, N, stride=slab), :] = plane


def line_kernel(in_ref, green_ref, left_ref, out_ref):
    groups, _, local, slab, _ = in_ref.shape
    for a in range(local):
        block = in_ref[:, 0, a].reshape(N, N)
        block = table_by_rows(left_ref[...], block) * green_ref[a]
        block = table_by_rows(left_ref[...], block)
        out_ref[:, 0, a] = block.reshape(groups, slab, N)


def gather_kernel(in_ref, phi_ref, orb_ref, left_ref, right_ref, applied_ref, owner_ref, lines):
    slab = orb_ref.shape[1]
    item, orbit = pl.program_id(0), pl.program_id(1)
    flat = in_ref.reshape(N * slab, N)
    for z in range(slab):
        plane = flat[pl.ds(z, N, stride=slab), :]
        lines[z * N:(z + 1) * N] = table_by_rows(left_ref[...], plane)
    result = rows_by_table(lines[...], right_ref[...]).reshape(slab, N, N) * MIX
    applied = result * phi_ref[0]
    owner = result * orb_ref[0]

    @pl.when(item == 0)
    def _():
        applied_ref[orbit] = applied

    @pl.when(item > 0)
    def _():
        applied_ref[orbit] += applied

    @pl.when(orbit == 0)
    def _():
        owner_ref[0] = owner

    @pl.when(orbit > 0)
    def _():
        owner_ref[0] += owner


def params():
    return pltpu.CompilerParams(vmem_limit_bytes=VMEM)


def whole(array):
    return pl.BlockSpec(array.shape, lambda *_: (0,) * array.ndim)


def spread(phi, orbitals, left, right, groups):
    items, slab = phi.shape[:2]
    count = orbitals.shape[0]
    local = N // groups
    fields = items * count
    return pl.pallas_call(
        spread_kernel,
        grid=(items, count),
        out_shape=jax.ShapeDtypeStruct((groups, fields, local, slab, N), jnp.float32),
        in_specs=[
            pl.BlockSpec((1, slab, N, N), lambda i, j: (i, 0, 0, 0)),
            pl.BlockSpec((1, slab, N, N), lambda i, j: (j, 0, 0, 0)),
            whole(left),
            whole(right),
        ],
        out_specs=pl.BlockSpec((groups, 1, local, slab, N), lambda i, j: (0, i * count + j, 0, 0, 0)),
        compiler_params=params(),
        cost_estimate=pl.CostEstimate(flops=fields * slab * N * N * 4096, bytes_accessed=fields * slab * N * N * 12, transcendentals=0),
    )(phi, orbitals, left, right)


def lines(field, green, left):
    groups, fields, local, slab, _ = field.shape
    block = pl.BlockSpec((groups, 1, local, slab, N), lambda f: (0, f, 0, 0, 0))
    return pl.pallas_call(
        line_kernel,
        grid=(fields,),
        out_shape=jax.ShapeDtypeStruct(field.shape, jnp.float32),
        in_specs=[block, whole(green), whole(left)],
        out_specs=block,
        compiler_params=params(),
        cost_estimate=pl.CostEstimate(flops=fields * slab * N * N * 4096, bytes_accessed=fields * slab * N * N * 12, transcendentals=0),
    )(field, green, left)


def collect(field, phi, orbitals, left, right):
    groups, fields, local, slab, _ = field.shape
    items, count = phi.shape[0], orbitals.shape[0]
    return pl.pallas_call(
        gather_kernel,
        grid=(items, count),
        out_shape=(
            jax.ShapeDtypeStruct(orbitals.shape, jnp.float32),
            jax.ShapeDtypeStruct(phi.shape, jnp.float32),
        ),
        in_specs=[
            pl.BlockSpec((groups, 1, local, slab, N), lambda i, j: (0, i * count + j, 0, 0, 0)),
            pl.BlockSpec((1, slab, N, N), lambda i, j: (i, 0, 0, 0)),
            pl.BlockSpec((1, slab, N, N), lambda i, j: (j, 0, 0, 0)),
            whole(left),
            whole(right),
        ],
        out_specs=(
            pl.BlockSpec(orbitals.shape, lambda i, j: (0, 0, 0, 0)),
            pl.BlockSpec((1, slab, N, N), lambda i, j: (i, 0, 0, 0)),
        ),
        scratch_shapes=[pltpu.VMEM((slab * N, N), jnp.float32)],
        compiler_params=params(),
        cost_estimate=pl.CostEstimate(flops=fields * slab * N * N * 4096, bytes_accessed=fields * slab * N * N * 16, transcendentals=0),
    )(field, phi, orbitals, left, right)


def wavenumber(idx):
    shifted = jnp.where(idx < N // 2, idx, idx - N)
    return 2.0 * math.pi / (N * SPACING) * shifted.astype(jnp.float32)


def green_table(groups):
    local = N // groups
    every = jnp.arange(N, dtype=jnp.int32)
    g_y = wavenumber(lax.axis_index("fft") * local + jnp.arange(local, dtype=jnp.int32))[:, None, None]
    g_z = wavenumber(every)[None, :, None]
    g_x = wavenumber(every)[None, None, :]
    ratio = (g_z * g_z + g_y * g_y + g_x * g_x) / (4.0 * OMEGA * OMEGA)
    safe = jnp.where(ratio > 0, ratio, 1.0)
    kernel = math.pi / (OMEGA * OMEGA) * jnp.where(ratio > 0, -jnp.expm1(-safe) / safe, 1.0)
    return kernel * (1.0 / N**3)


def sent_orbitals(orbitals):
    band = lax.axis_index("band")
    ring = band // 2
    zero = jnp.zeros_like(orbitals[0])
    parts = []
    for item in range(orbitals.shape[0]):
        own = orbitals[item]
        near = jnp.where(band == 0, own, zero)
        far = jnp.where(band == 8, own, zero)
        send = lax.ppermute(own, "band", [(0, 1), (8, 9)])
        near = near + jnp.where(ring == 0, send, zero)
        far = far + jnp.where(ring == 4, send, zero)
        for step in range(1, 5):
            up = []
            down = []
            for y in range(2):
                for start in (0, 4):
                    up.append(((start + step - 1) % 8 * 2 + y, (start + step) % 8 * 2 + y))
                    down.append(((start - step + 1) % 8 * 2 + y, (start - step) % 8 * 2 + y))
            got = lax.ppermute(jnp.where(ring < 4, near, far), "band", up)
            low_end = (ring >= 1) & (ring <= 4)
            if step < 4:
                back = lax.ppermute(jnp.where((ring > 4) | (ring == 0), near, far), "band", down)
                near = near + jnp.where(low_end, got, back)
                far = far + jnp.where(low_end, back, got)
            else:
                near = near + jnp.where(low_end, got, zero)
                far = far + jnp.where(low_end, zero, got)
        parts.append((near, far))
    return [parts[0][0], parts[1][0], parts[0][1], parts[1][1]]


def swap(array, axis):
    return lax.all_to_all(array, axis, split_axis=0, concat_axis=0)


def per_device(orbitals):
    groups, nband = lax.axis_size("fft"), lax.axis_size("band")
    left, right = (jnp.asarray(t) for t in cas_tables())
    green = green_table(groups)
    phis = sent_orbitals(orbitals)
    applied = None
    terms = []
    for chunk in range(2):
        phi = jnp.stack(phis[2 * chunk:2 * chunk + 2])
        field = spread(phi, orbitals, left, right, groups)
        field = lines(swap(field, "fft"), green, left)
        part, owner = collect(swap(field, "fft"), phi, orbitals, left, right)
        applied = part if applied is None else applied + part
        share = swap(owner.reshape(nband, 1, N, N), "band")
        share = jnp.sum(share, 0)
        every = swap(jnp.broadcast_to(share[None], (nband, 1, N, N)), "band")
        terms.append(every.reshape(owner.shape))
    return applied, jnp.concatenate(terms, 0)


def solution(mesh):
    return jax.shard_map(
        per_device,
        mesh=mesh,
        in_specs=(P("band", "fft", None, None),),
        out_specs=(P("band", "fft", None, None), P(None, "fft", None, None)),
        check_vma=False,
    )
```

```python
import functools
import math

import jax
import jax.numpy as jnp
import ml_dtypes
import numpy as np
from jax import lax
from jax.experimental import pallas as pl
from jax.experimental.pallas import tpu as pltpu
from jax.sharding import PartitionSpec as P

N = 128
SPACING = 0.29
OMEGA = 0.106
MIX = -0.25
VMEM = 48 * 1024 * 1024
GROUP = 8
SLAB = 8
LOCAL = N // GROUP


def split(full):
    high = full.astype(ml_dtypes.bfloat16)
    low = (full - high.astype(np.float64)).astype(ml_dtypes.bfloat16)
    return np.concatenate([high, low], -1)


def cas_tables():
    idx = np.arange(N)
    angle = 2.0 * np.pi / N * (idx[:, None] * idx[None, :] % N)
    full = np.cos(angle) + np.sin(angle)
    plain = split(full)
    right = np.concatenate([plain, plain], 0)
    y_order = [np.concatenate([(g ^ d) * LOCAL + np.arange(LOCAL) for d in range(GROUP)]) for g in range(GROUP)]
    z_order = [np.concatenate([(f ^ e) * SLAB + np.arange(SLAB) for e in range(2 * GROUP)]) for f in range(2 * GROUP)]
    to_y = np.stack([split(full[o]) for o in y_order])
    from_y = np.stack([split(full[:, o]) for o in y_order])
    to_z = np.stack([split(full[:, o]) for o in z_order])
    from_z = np.stack([split(full[o]) for o in z_order])
    return right, to_y, from_y, to_z, from_z


def halves(value):
    high = value.astype(jnp.bfloat16)
    low = (value - high.astype(jnp.float32)).astype(jnp.bfloat16)
    return high, low


def dot(a, b):
    return lax.dot_general(a, b, (((1,), (0,)), ((), ())), preferred_element_type=jnp.float32)


def rows_by_table(value, right):
    out = dot(jnp.concatenate(halves(value), 1), right)
    return out[:, :N] + out[:, N:]


def table_by_rows(left, value):
    pair = jnp.concatenate(halves(value), 1)
    out = dot(left, jnp.concatenate([pair, pair], 0))
    return out[:, :N] + out[:, N:]


def spread_kernel(phi_ref, first_ref, second_ref, to_y_ref, right_ref, *out_refs):
    for j, orb_ref in enumerate((first_ref, second_ref)):
        density = (phi_ref[...] * orb_ref[...]).reshape(SLAB * N, N)
        lines = rows_by_table(density, right_ref[...])
        for z in range(SLAB):
            plane = table_by_rows(to_y_ref[...], lines[z * N:(z + 1) * N])
            for d, out_ref in enumerate(out_refs):
                flat = out_ref.reshape(2 * LOCAL * SLAB, N)
                flat[pl.ds(j * LOCAL * SLAB + z, LOCAL, stride=SLAB), :] = plane[d * LOCAL:(d + 1) * LOCAL]


def line_kernel(*refs):
    count = 2 * GROUP
    in_refs, (green_ref, to_z_ref, from_z_ref), out_refs = refs[:count], refs[count:count + 3], refs[count + 3:]

    @pl.loop(0, LOCAL, unroll=4)
    def _(a):
        block = jnp.concatenate([ref[0, a] for ref in in_refs], 0)
        block = table_by_rows(to_z_ref[...], block) * green_ref[a]
        block = table_by_rows(from_z_ref[...], block)
        for e, ref in enumerate(out_refs):
            ref[0, a] = block[e * SLAB:(e + 1) * SLAB]


def gather_kernel(with_sum, *refs):
    in_refs, refs = refs[:GROUP], refs[GROUP:]
    phi_ref, first_ref, second_ref, from_y_ref, right_ref = refs[:5]
    sums, refs = (refs[5:7], refs[7:]) if with_sum else (None, refs[5:])
    out_refs, owner_ref, lines = refs[:2], refs[2], refs[3]
    for j, orb_ref in enumerate((first_ref, second_ref)):
        for z in range(SLAB):
            rows = pl.ds(j * LOCAL * SLAB + z, LOCAL, stride=SLAB)
            plane = jnp.concatenate([ref.reshape(2 * LOCAL * SLAB, N)[rows, :] for ref in in_refs], 0)
            lines[z * N:(z + 1) * N] = table_by_rows(from_y_ref[...], plane)
        result = rows_by_table(lines[...], right_ref[...]).reshape(SLAB, N, N) * MIX
        applied = result * phi_ref[...]
        out_refs[j][...] = applied + sums[j][...] if with_sum else applied
        owner = result * orb_ref[...]
        owner_ref[...] = owner if j == 0 else owner_ref[...] + owner


def params():
    return pltpu.CompilerParams(vmem_limit_bytes=VMEM)


def cost(planes):
    return pl.CostEstimate(flops=planes * N * N * 2048, bytes_accessed=planes * N * N * 12, transcendentals=0)


SLAB_SHAPE = jax.ShapeDtypeStruct((SLAB, N, N), jnp.float32)
PART_SHAPE = jax.ShapeDtypeStruct((2, LOCAL, SLAB, N), jnp.float32)


def spread(phi, pair, to_y, right):
    return pl.pallas_call(
        spread_kernel,
        out_shape=(PART_SHAPE,) * GROUP,
        compiler_params=params(),
        cost_estimate=cost(2 * SLAB),
    )(phi, *pair, to_y, right)


def lines(parts, green, to_z, from_z):
    block = pl.BlockSpec((1, LOCAL, SLAB, N), lambda j: (j, 0, 0, 0))

    def whole(array):
        return pl.BlockSpec(array.shape, lambda j: (0,) * array.ndim)

    return pl.pallas_call(
        line_kernel,
        grid=(2,),
        out_shape=(PART_SHAPE,) * len(parts),
        in_specs=[block] * len(parts) + [whole(green), whole(to_z), whole(from_z)],
        out_specs=(block,) * len(parts),
        compiler_params=params(),
        cost_estimate=cost(8 * SLAB),
    )(*parts, green, to_z, from_z)


def collect(parts, phi, pair, from_y, right, sums):
    return pl.pallas_call(
        functools.partial(gather_kernel, sums is not None),
        out_shape=(SLAB_SHAPE,) * 3,
        scratch_shapes=[pltpu.VMEM((SLAB * N, N), jnp.float32)],
        compiler_params=params(),
        cost_estimate=cost(2 * SLAB),
    )(*parts, phi, *pair, from_y, right, *(sums or ()))


def wavenumber(idx):
    shifted = jnp.where(idx < N // 2, idx, idx - N)
    return 2.0 * math.pi / (N * SPACING) * shifted.astype(jnp.float32)


def green_table(group):
    every = jnp.arange(N, dtype=jnp.int32)
    g_y = wavenumber(group * LOCAL + jnp.arange(LOCAL, dtype=jnp.int32))[:, None, None]
    g_z = wavenumber(every)[None, :, None]
    g_x = wavenumber(every)[None, None, :]
    ratio = (g_z * g_z + g_y * g_y + g_x * g_x) / (4.0 * OMEGA * OMEGA)
    safe = jnp.where(ratio > 0, ratio, 1.0)
    kernel = math.pi / (OMEGA * OMEGA) * jnp.where(ratio > 0, -jnp.expm1(-safe) / safe, 1.0)
    return kernel * (1.0 / N**3)


def band_pairs(y_hi, moves):
    return [(2 * a + y_hi, 2 * b + y_hi) for a, b in moves]


def over_y(array):
    return lax.ppermute(array, "fft", [(i, i ^ GROUP) for i in range(2 * GROUP)])


def exchange(parts):
    return [
        part if d == 0 else lax.ppermute(part, "fft", [(i, i ^ d) for i in range(2 * GROUP)])
        for d, part in enumerate(parts)
    ]


def cross(piece, band):
    other = lax.ppermute(piece, "band", [(0, 8), (8, 0)])
    return jnp.where(band == 0, piece, other), jnp.where(band == 8, piece, other)


def chain(piece):
    up = lax.ppermute(piece, "band", band_pairs(0, [(0, 1), (4, 5)]))
    down = lax.ppermute(piece, "band", band_pairs(0, [(0, 7), (4, 3)]))
    next_down = lax.ppermute(down, "band", band_pairs(0, [(7, 6), (3, 2)]))
    ring = piece + up + down + next_down
    return ring + lax.ppermute(ring, "band", [(2 * z, 2 * z + 1) for z in range(8)])


def swap_z(array):
    groups = [[2 * z + y for z in range(8)] for y in range(2)]
    return lax.all_to_all(array, "band", 0, 0, axis_index_groups=groups)


def over_y_hi(array):
    return lax.ppermute(array, "band", [(b, b ^ 1) for b in range(16)])


def total(own, far, band):
    y_hi = band % 2
    half = SLAB // 2
    both = jnp.stack([own, far]).reshape(2, 2, half, N, N)
    keep = jnp.where(y_hi == 0, both[:, 0], both[:, 1])
    give = jnp.where(y_hi == 0, both[:, 1], both[:, 0])
    keep = keep + over_y_hi(give)
    size = half * N // 8
    keep = jnp.swapaxes(keep.reshape(2, 8, size, N), 0, 1)
    share = jnp.sum(swap_z(keep), 0)
    share = jnp.stack([share[0], over_y(share[1])])
    mine = swap_z(jnp.broadcast_to(share[None], (8,) + share.shape))
    mine = jnp.swapaxes(mine, 0, 1).reshape(2, half, N, N)
    other = over_y_hi(mine)
    low = jnp.where(y_hi == 0, mine, other)
    high = jnp.where(y_hi == 0, other, mine)
    return jnp.concatenate([low, high], 1)


def per_device(orbitals):
    place, band = lax.axis_index("fft"), lax.axis_index("band")
    y_lo, group = place // GROUP, place % GROUP
    right, to_y, from_y, to_z, from_z = cas_tables()
    right = jnp.asarray(right)
    to_y, from_y = (lax.dynamic_index_in_dim(jnp.asarray(t), group, 0, False) for t in (to_y, from_y))
    to_z, from_z = (lax.dynamic_index_in_dim(jnp.asarray(t), place, 0, False) for t in (to_z, from_z))
    green = green_table(group)
    low = y_lo == 0

    own = (jnp.where(low, orbitals[0], orbitals[1]), jnp.where(low, orbitals[1], orbitals[0]))
    far = (over_y(own[1]), over_y(own[0]))
    pairs = (own, far)
    half = SLAB // 2
    sent = [[], []]
    for pair in pairs:
        pieces = [cross(pair[0][k * half:(k + 1) * half], band) for k in range(2)]
        for owner in range(2):
            sent[owner].append(jnp.concatenate([chain(piece[owner]) for piece in pieces], 0))

    fields = []
    for owner in range(2):
        parts = []
        for phi, pair in zip(sent[owner], pairs):
            parts += exchange(spread(phi, pair, to_y, right))
        fields.append(lines(parts, green, to_z, from_z))
    sums = [None, None]
    terms = []
    for owner in range(2):
        found = [None, None]
        for p in (1, 0):
            parts = exchange(fields[owner][p * GROUP:(p + 1) * GROUP])
            *sums[p], found[p] = collect(parts, sent[owner][p], pairs[p], from_y, right, sums[p])
        terms.append(total(found[0], found[1], band))
    back = [over_y(part) for part in sums[1]]
    first, second = sums[0][0] + back[1], sums[0][1] + back[0]
    applied = jnp.stack([jnp.where(low, first, second), jnp.where(low, second, first)])
    owner_terms = jnp.concatenate([jnp.where(low, t, t[::-1]) for t in terms], 0)
    return applied, owner_terms


def solution(mesh):
    return jax.shard_map(
        per_device,
        mesh=mesh,
        in_specs=(P("band", "fft", None, None),),
        out_specs=(P("band", "fft", None, None), P(None, "fft", None, None)),
        check_vma=False,
    )
```

```python
import functools
import math

import jax
import jax.numpy as jnp
import ml_dtypes
import numpy as np
from jax import lax
from jax.experimental import pallas as pl
from jax.experimental.pallas import tpu as pltpu
from jax.sharding import PartitionSpec as P

N = 128
SPACING = 0.29
OMEGA = 0.106
MIX = -0.25
VMEM = 32 * 1024 * 1024
SLAB = 8
PLANES = 4
ORBS = 4
SENT = 4
FIELDS = ORBS * SENT
GROUP = 32
LOCAL = N // GROUP


def split(full):
    high = full.astype(ml_dtypes.bfloat16)
    low = (full - high.astype(np.float64)).astype(ml_dtypes.bfloat16)
    return np.concatenate([high, low], -1)


def cas_tables():
    idx = np.arange(N)
    angle = 2.0 * np.pi / N * (idx[:, None] * idx[None, :] % N)
    full = np.cos(angle) + np.sin(angle)
    left = split(full)
    right = np.concatenate([left, left], 0)
    order = np.array([(2 * chip + c) * SLAB + 2 * q + p for c in range(2) for p in range(2) for chip in range(8) for q in range(4)])
    return left, right, split(full[:, order]), split(full[order])


def halves(value):
    high = value.astype(jnp.bfloat16)
    low = (value - high.astype(jnp.float32)).astype(jnp.bfloat16)
    return high, low


def dot(a, b):
    return lax.dot_general(a, b, (((1,), (0,)), ((), ())), preferred_element_type=jnp.float32)


def rows_by_table(value, right):
    out = dot(jnp.concatenate(halves(value), 1), right)
    return out[:, :N] + out[:, N:]


def table_by_rows(left, value):
    pair = jnp.concatenate(halves(value), 1)
    out = dot(left, jnp.concatenate([pair, pair], 0))
    return out[:, :N] + out[:, N:]


def spread_kernel(phi_ref, orb_ref, left_ref, right_ref, out_ref):
    item, orbit = pl.program_id(0), pl.program_id(1)
    flat = out_ref.reshape(N * PLANES, N)
    density = [phi_ref[item, c, p] * orb_ref[c, orbit, p] for c in range(2) for p in range(2)]
    lines = rows_by_table(jnp.concatenate(density, 0), right_ref[...])
    for z in range(PLANES):
        flat[pl.ds(z, N, stride=PLANES), :] = table_by_rows(left_ref[...], lines[z * N:(z + 1) * N])


def line_kernel(in_ref, green_ref, to_z_ref, from_z_ref, out_ref):
    given, taken = (ref.reshape(GROUP * LOCAL * PLANES, N) for ref in (in_ref, out_ref))
    for a in range(LOCAL):
        rows = [pl.ds(a * PLANES + z, GROUP, stride=LOCAL * PLANES) for z in range(PLANES)]
        block = jnp.concatenate([given[r, :] for r in rows], 0)
        block = table_by_rows(to_z_ref[...], block) * green_ref[a]
        block = table_by_rows(from_z_ref[...], block)
        for z, r in enumerate(rows):
            taken[r, :] = block[z * GROUP:(z + 1) * GROUP]


def gather_kernel(in_ref, phi_ref, orb_ref, left_ref, right_ref, applied_ref, owner_ref, lines):
    item, orbit = pl.program_id(0), pl.program_id(1)
    flat = in_ref.reshape(N * PLANES, N)
    for z in range(PLANES):
        lines[z * N:(z + 1) * N] = table_by_rows(left_ref[...], flat[pl.ds(z, N, stride=PLANES), :])
    result = rows_by_table(lines[...], right_ref[...]) * MIX
    for c in range(2):
        for p in range(2):
            plane = result[(2 * c + p) * N:(2 * c + p + 1) * N]
            applied = plane * phi_ref[item, c, p]
            owner = plane * orb_ref[c, orbit, p]

            @pl.when(item == 0)
            def _():
                applied_ref[c, orbit, p] = applied

            @pl.when(item > 0)
            def _():
                applied_ref[c, orbit, p] += applied

            @pl.when(orbit == 0)
            def _():
                owner_ref[c, item, p] = owner

            @pl.when(orbit > 0)
            def _():
                owner_ref[c, item, p] += owner


def params():
    return pltpu.CompilerParams(vmem_limit_bytes=VMEM)


def cost(planes):
    return pl.CostEstimate(flops=planes * N * N * 2048, bytes_accessed=planes * N * N * 12, transcendentals=0)


FIELD_SHAPE = jax.ShapeDtypeStruct((GROUP, FIELDS, LOCAL * PLANES, N), jnp.float32)
FIELD_BLOCK = pl.BlockSpec((GROUP, 1, LOCAL * PLANES, N), lambda i, j: (0, ORBS * i + j, 0, 0))


def whole(array):
    return pl.BlockSpec(array.shape, lambda *_: (0,) * array.ndim)


def spread(phi, orbs, left, right):
    given = (phi, orbs, left, right)
    return pl.pallas_call(
        spread_kernel,
        grid=(SENT, ORBS),
        out_shape=FIELD_SHAPE,
        in_specs=[whole(array) for array in given],
        out_specs=FIELD_BLOCK,
        compiler_params=params(),
        cost_estimate=cost(FIELDS * PLANES),
    )(*given)


def lines(field, green, to_z, from_z):
    return pl.pallas_call(
        line_kernel,
        grid=(SENT, ORBS),
        out_shape=FIELD_SHAPE,
        in_specs=[FIELD_BLOCK, whole(green), whole(to_z), whole(from_z)],
        out_specs=FIELD_BLOCK,
        compiler_params=params(),
        cost_estimate=cost(FIELDS * PLANES),
    )(field, green, to_z, from_z)


def collect(field, phi, orbs, left, right):
    given = (phi, orbs, left, right)
    shapes = (jax.ShapeDtypeStruct(orbs.shape, jnp.float32), jax.ShapeDtypeStruct((2, SENT, 2, N, N), jnp.float32))
    return pl.pallas_call(
        gather_kernel,
        grid=(SENT, ORBS),
        out_shape=shapes,
        in_specs=[FIELD_BLOCK] + [whole(array) for array in given],
        out_specs=tuple(whole(shape) for shape in shapes),
        scratch_shapes=[pltpu.VMEM((PLANES * N, N), jnp.float32)],
        compiler_params=params(),
        cost_estimate=cost(FIELDS * PLANES),
    )(field, *given)


def wavenumber(idx):
    shifted = jnp.where(idx < N // 2, idx, idx - N)
    return 2.0 * math.pi / (N * SPACING) * shifted.astype(jnp.float32)


def green_table(group):
    every = jnp.arange(N, dtype=jnp.int32)
    g_y = wavenumber(group * LOCAL + jnp.arange(LOCAL, dtype=jnp.int32))[:, None, None]
    g_z = wavenumber(every)[None, :, None]
    g_x = wavenumber(every)[None, None, :]
    ratio = (g_z * g_z + g_y * g_y + g_x * g_x) / (4.0 * OMEGA * OMEGA)
    safe = jnp.where(ratio > 0, ratio, 1.0)
    kernel = math.pi / (OMEGA * OMEGA) * jnp.where(ratio > 0, -jnp.expm1(-safe) / safe, 1.0)
    return kernel * (1.0 / N**3)


def over_core(array):
    return lax.ppermute(array, "fft", [(i, i ^ 1) for i in range(16)])


EVERY = ("band", "fft")
POOL_CORES = [
    [(4 * pool + k) * 16 + 2 * chip + c for c in range(2) for k in range(4)] for pool in range(4) for chip in range(8)
]
LINES = [[(4 * pool + k) * 16 + 2 * chip + c for chip in range(8) for k in range(4)] for pool in range(4) for c in range(2)]
POOLS = [[4 * pool + k for k in range(4)] for pool in range(4)]
ACROSS = [[4 * pool + k for pool in range(4)] for k in range(4)]


def swap(array, axis, groups):
    return lax.all_to_all(array, axis, 0, 0, axis_index_groups=groups)


def spread_out(array, axis, groups):
    return swap(jnp.broadcast_to(array[None], (4,) + array.shape), axis, groups)


def to_pools(array, moves):
    return lax.ppermute(array, "band", [(4 * a + k, 4 * b + k) for a, b in moves for k in range(4)])


def per_device(orbitals):
    place, band = lax.axis_index("fft"), lax.axis_index("band")
    core, pool = place % 2, band // 4
    left, right, to_z, from_z = (jnp.asarray(t) for t in cas_tables())
    green = green_table(place // 2 * 4 + band % 4)

    orbs = swap(orbitals.reshape(8, 2, N, N), EVERY, POOL_CORES).reshape(2, ORBS, 2, N, N)
    near = orbs[:, 0]
    across = to_pools(near, [(0, 2), (2, 0)])
    above = to_pools(near, [(0, 1), (2, 3)])
    below = to_pools(near, [(0, 3), (2, 1)])

    def pick(*options):
        return lax.select_n(pool, *options)

    mine = jnp.stack([pick(near, above, across, below), pick(across, below, near, above)])
    other = over_core(mine)
    phi = jnp.stack([jnp.where(core == 0, mine, other), jnp.where(core == 0, other, mine)], 1)
    phi = phi.reshape((SENT,) + phi.shape[2:])

    field = swap(spread(phi, orbs, left, right), EVERY, LINES)
    field = swap(lines(field, green, to_z, from_z), EVERY, LINES)
    applied, owner = collect(field, phi, orbs, left, right)

    owner = jnp.where(core == 0, owner[0], owner[1]) + over_core(jnp.where(core == 0, owner[1], owner[0]))
    owner = jnp.sum(swap(owner, "band", ACROSS), 0)
    terms = spread_out(spread_out(owner, "band", ACROSS), "band", POOLS)
    terms = jnp.swapaxes(terms, 0, 1).reshape(SENT, SLAB, N, N)
    applied = swap(applied.reshape(8, 2, N, N), EVERY, POOL_CORES).reshape(orbitals.shape)
    return applied, terms


def solution(mesh):
    return jax.shard_map(
        per_device,
        mesh=mesh,
        in_specs=(P("band", "fft", None, None),),
        out_specs=(P("band", "fft", None, None), P(None, "fft", None, None)),
        check_vma=False,
    )
```

```python
import functools
import math

import jax
import jax.numpy as jnp
import ml_dtypes
import numpy as np
from jax import lax
from jax.experimental import pallas as pl
from jax.experimental.pallas import tpu as pltpu
from jax.sharding import PartitionSpec as P

N = 128
SPACING = 0.29
OMEGA = 0.106
MIX = -0.25
VMEM = 32 * 1024 * 1024
SLAB = 8
PLANES = 4
ORBS = 4
SENT = 4
GROUP = 32
LOCAL = N // GROUP
ROWS = ORBS * PLANES


def split(full):
    high = full.astype(ml_dtypes.bfloat16)
    low = (full - high.astype(np.float64)).astype(ml_dtypes.bfloat16)
    return np.concatenate([high, low], -1)


def cas_tables():
    idx = np.arange(N)
    angle = 2.0 * np.pi / N * (idx[:, None] * idx[None, :] % N)
    full = np.cos(angle) + np.sin(angle)
    order = np.array([(2 * chip + c) * SLAB + 2 * q + p for c in range(2) for p in range(2) for chip in range(8) for q in range(4)])
    return [np.concatenate([split(t)] * 2, 0) for t in (full, full[order], full[:, order])]


def halves(value):
    high = value.astype(jnp.bfloat16)
    low = (value - high.astype(jnp.float32)).astype(jnp.bfloat16)
    return high, low


def dot(a, b):
    return lax.dot_general(a, b, (((1,), (0,)), ((), ())), preferred_element_type=jnp.float32)


def rows_by_table(value, right):
    out = dot(jnp.concatenate(halves(value), 1), right)
    return out[:, :N] + out[:, N:]


def turned(value):
    return jnp.concatenate([value[r:r + N].T for r in range(0, value.shape[0], N)], 0)


def spread_kernel(phi_ref, orb_ref, table_ref, out_ref):
    flat = out_ref.reshape(N * ROWS, N)
    for j in range(ORBS):
        density = [phi_ref[0, c, p] * orb_ref[c, j, p] for c in range(2) for p in range(2)]
        field = turned(rows_by_table(jnp.concatenate(density, 0), table_ref[...]))
        field = rows_by_table(field, table_ref[...])
        for z in range(PLANES):
            flat[pl.ds(j * PLANES + z, N, stride=ROWS), :] = field[z * N:(z + 1) * N]


def line_kernel(in_ref, green_ref, to_z_ref, from_z_ref, out_ref):
    given, taken = (ref.reshape(N * ROWS, N) for ref in (in_ref, out_ref))
    for a in range(LOCAL):
        rows = [pl.ds(a * ROWS + r, GROUP, stride=LOCAL * ROWS) for r in range(ROWS)]
        field = turned(jnp.concatenate([given[r, :] for r in rows], 0))
        field = rows_by_table(field, to_z_ref[...]).reshape(ORBS, N, N) * green_ref[a]
        field = turned(rows_by_table(field.reshape(ORBS * N, N), from_z_ref[...]))
        for z, r in enumerate(rows):
            taken[r, :] = field[z * GROUP:(z + 1) * GROUP]


def gather_kernel(in_ref, phi_ref, orb_ref, table_ref, applied_ref, owner_ref):
    item = pl.program_id(0)
    flat = in_ref.reshape(N * ROWS, N)
    owner = None
    for j in range(ORBS):
        field = jnp.concatenate([flat[pl.ds(j * PLANES + z, N, stride=ROWS), :] for z in range(PLANES)], 0)
        field = turned(rows_by_table(field, table_ref[...]))
        result = (rows_by_table(field, table_ref[...]) * MIX).reshape(2, 2, N, N)
        applied = result * phi_ref[0]
        part = result * orb_ref[:, j]
        owner = part if j == 0 else owner + part

        @pl.when(item == 0)
        def _():
            applied_ref[:, j] = applied

        @pl.when(item > 0)
        def _():
            applied_ref[:, j] += applied

    owner_ref[0] = owner


def params():
    return pltpu.CompilerParams(vmem_limit_bytes=VMEM)


def cost(planes):
    return pl.CostEstimate(flops=planes * N * N * 2048, bytes_accessed=planes * N * N * 12, transcendentals=0)


FIELD_SHAPE = jax.ShapeDtypeStruct((GROUP, SENT, LOCAL * ROWS, N), jnp.float32)
FIELD_BLOCK = pl.BlockSpec((GROUP, 1, LOCAL * ROWS, N), lambda i: (0, i, 0, 0))
SENT_BLOCK = pl.BlockSpec((1, 2, 2, N, N), lambda i: (i, 0, 0, 0, 0))


def whole(array):
    return pl.BlockSpec(array.shape, lambda *_: (0,) * array.ndim)


def spread(phi, orbs, table):
    given = (phi, orbs, table)
    return pl.pallas_call(
        spread_kernel,
        grid=(SENT,),
        out_shape=FIELD_SHAPE,
        in_specs=[SENT_BLOCK] + [whole(array) for array in given[1:]],
        out_specs=FIELD_BLOCK,
        compiler_params=params(),
        cost_estimate=cost(SENT * ROWS),
    )(*given)


def lines(field, green, to_z, from_z):
    return pl.pallas_call(
        line_kernel,
        grid=(SENT,),
        out_shape=FIELD_SHAPE,
        in_specs=[FIELD_BLOCK, whole(green), whole(to_z), whole(from_z)],
        out_specs=FIELD_BLOCK,
        compiler_params=params(),
        cost_estimate=cost(SENT * ROWS),
    )(field, green, to_z, from_z)


def collect(field, phi, orbs, table):
    given = (phi, orbs, table)
    shapes = (jax.ShapeDtypeStruct(orbs.shape, jnp.float32), jax.ShapeDtypeStruct((SENT, 2, 2, N, N), jnp.float32))
    return pl.pallas_call(
        gather_kernel,
        grid=(SENT,),
        out_shape=shapes,
        in_specs=[FIELD_BLOCK, SENT_BLOCK] + [whole(array) for array in given[1:]],
        out_specs=(whole(shapes[0]), SENT_BLOCK),
        compiler_params=params(),
        cost_estimate=cost(SENT * ROWS),
    )(field, *given)


def wavenumber(idx):
    shifted = jnp.where(idx < N // 2, idx, idx - N)
    return 2.0 * math.pi / (N * SPACING) * shifted.astype(jnp.float32)


def green_table(group):
    every = jnp.arange(N, dtype=jnp.int32)
    g_y = wavenumber(group * LOCAL + jnp.arange(LOCAL, dtype=jnp.int32))[:, None, None]
    g_z = wavenumber(every)[None, :, None]
    g_x = wavenumber(every)[None, None, :]
    ratio = (g_z * g_z + g_y * g_y + g_x * g_x) / (4.0 * OMEGA * OMEGA)
    safe = jnp.where(ratio > 0, ratio, 1.0)
    kernel = math.pi / (OMEGA * OMEGA) * jnp.where(ratio > 0, -jnp.expm1(-safe) / safe, 1.0)
    return kernel * (1.0 / N**3)


def over_core(array):
    return lax.ppermute(array, "fft", [(i, i ^ 1) for i in range(16)])


EVERY = ("band", "fft")
POOL_CORES = [
    [(4 * pool + k) * 16 + 2 * chip + c for c in range(2) for k in range(4)] for pool in range(4) for chip in range(8)
]
LINES = [[(4 * pool + k) * 16 + 2 * chip + c for chip in range(8) for k in range(4)] for pool in range(4) for c in range(2)]
POOLS = [[4 * pool + k for k in range(4)] for pool in range(4)]
ACROSS = [[4 * pool + k for pool in range(4)] for k in range(4)]


def swap(array, axis, groups):
    return lax.all_to_all(array, axis, 0, 0, axis_index_groups=groups)


def spread_out(array, axis, groups):
    return swap(jnp.broadcast_to(array[None], (4,) + array.shape), axis, groups)


def to_pools(array, moves):
    return lax.ppermute(array, "band", [(4 * a + k, 4 * b + k) for a, b in moves for k in range(4)])


def per_device(orbitals):
    place, band = lax.axis_index("fft"), lax.axis_index("band")
    core, pool = place % 2, band // 4
    table, to_z, from_z = (jnp.asarray(t) for t in cas_tables())
    green = green_table(place // 2 * 4 + band % 4)

    orbs = swap(orbitals.reshape(8, 2, N, N), EVERY, POOL_CORES).reshape(2, ORBS, 2, N, N)
    near = orbs[:, 0]
    across = to_pools(near, [(0, 2), (2, 0)])
    above = to_pools(near, [(0, 1), (2, 3)])
    below = to_pools(near, [(0, 3), (2, 1)])

    def pick(*options):
        return lax.select_n(pool, *options)

    mine = jnp.stack([pick(near, above, across, below), pick(across, below, near, above)])
    other = over_core(mine)
    phi = jnp.stack([jnp.where(core == 0, mine, other), jnp.where(core == 0, other, mine)], 1)
    phi = phi.reshape((SENT,) + phi.shape[2:])

    phi, green, to_z, from_z = lax.optimization_barrier((phi, green, to_z, from_z))
    field = swap(spread(phi, orbs, table), EVERY, LINES)
    field = swap(lines(field, green, to_z, from_z), EVERY, LINES)
    applied, owner = collect(field, phi, orbs, table)

    owner = owner.reshape(2, 2, 2, 2, N, N)
    owner = jnp.where(core == 0, owner[0], owner[1]) + over_core(jnp.where(core == 0, owner[1], owner[0]))
    owner = jnp.sum(swap(jnp.swapaxes(owner, 0, 1).reshape(4, 2, N, N), "band", ACROSS), 0)
    owner = spread_out(owner, "band", ACROSS).reshape(2, 1, 4, N, N)
    both = jnp.concatenate([applied, jnp.broadcast_to(owner, (2, ORBS, 4, N, N))], 2)
    both = swap(both.reshape(8, 6, N, N), EVERY, POOL_CORES)
    applied = both[:, :2].reshape(orbitals.shape)
    terms = both[:, 2:].reshape(2, 4, 2, 2, N, N)
    return applied, jnp.swapaxes(terms, 1, 2).reshape(SENT, SLAB, N, N)


def solution(mesh):
    return jax.shard_map(
        per_device,
        mesh=mesh,
        in_specs=(P("band", "fft", None, None),),
        out_specs=(P("band", "fft", None, None), P(None, "fft", None, None)),
        check_vma=False,
    )
```

```python
import functools
import math

import jax
import jax.numpy as jnp
import ml_dtypes
import numpy as np
from jax import lax
from jax.experimental import pallas as pl
from jax.experimental.pallas import tpu as pltpu
from jax.sharding import PartitionSpec as P

N = 128
SPACING = 0.29
OMEGA = 0.106
MIX = -0.25
VMEM = 32 * 1024 * 1024
SLAB = 8
PLANES = 4
ORBS = 4
SENT = 4
GROUP = 32
LOCAL = N // GROUP
ROWS = ORBS * PLANES


def split(full):
    high = full.astype(ml_dtypes.bfloat16)
    low = (full - high.astype(np.float64)).astype(ml_dtypes.bfloat16)
    return np.concatenate([high, low], -1)


def cas_tables():
    idx = np.arange(N)
    angle = 2.0 * np.pi / N * (idx[:, None] * idx[None, :] % N)
    full = np.cos(angle) + np.sin(angle)
    to_z = np.zeros((2, 2 * N, 2, N))
    for c in range(2):
        held = [
            (j, (2 * chip + (c ^ q)) * SLAB + 2 * k + p)
            for chip in range(8) for k in range(4) for j in range(2) for q in range(2) for p in range(2)
        ]
        for row, (j, z) in enumerate(held):
            to_z[c, row, j] = full[z]
    to_z = to_z.reshape(2, 2 * N, 2 * N)
    pairs = [np.stack(np.split(split(t), 2, -1), 1) for t in (to_z, to_z.transpose(0, 2, 1))]
    return [np.concatenate([split(full)] * 2, 0)] + pairs


def halves(value):
    high = value.astype(jnp.bfloat16)
    low = (value - high.astype(jnp.float32)).astype(jnp.bfloat16)
    return high, low


def dot(a, b):
    return lax.dot_general(a, b, (((1,), (0,)), ((), ())), preferred_element_type=jnp.float32)


def rows_by_table(value, right):
    out = dot(jnp.concatenate(halves(value), 1), right)
    return out[:, :N] + out[:, N:]


def turned(value):
    return jnp.concatenate([value[r:r + N].T for r in range(0, value.shape[0], N)], 0)


def spread_kernel(phi_ref, phi_beside_ref, orb_ref, orb_beside_ref, table_ref, out_ref):
    fields = []
    for j in range(ORBS):
        density = [phi_ref[0, p] * orb_ref[j, p] for p in range(2)]
        density += [phi_beside_ref[0, p] * orb_beside_ref[j, p] for p in range(2)]
        field = turned(rows_by_table(jnp.concatenate(density, 0), table_ref[...]))
        fields.append(rows_by_table(field, table_ref[...]).reshape(PLANES, N, N))
    for j in range(0, ORBS, 2):
        pair = jnp.swapaxes(jnp.concatenate(fields[j:j + 2], 0), 0, 1)
        out_ref[:, 0, :, j // 2] = pair.reshape(GROUP, LOCAL, 2 * PLANES, N)


def dot3(value, high, low):
    first, second = halves(value)
    return dot(first, high) + dot(second, high) + dot(first, low)


def line_kernel(in_ref, green_ref, to_z_ref, from_z_ref, out_ref):
    for a in range(LOCAL):
        green = jnp.concatenate([green_ref[a]] * 2, 1)
        for j in range(ORBS // 2):
            field = in_ref[:, 0, a, j].reshape(2 * N, N)
            field = jnp.concatenate([field[:N].T, field[N:].T], 1)
            field = dot3(field, to_z_ref[0], to_z_ref[1]) * green
            field = dot3(field, from_z_ref[0], from_z_ref[1])
            field = jnp.concatenate([field[:, :N].T, field[:, N:].T], 0)
            out_ref[:, 0, a, j] = field.reshape(GROUP, 2 * PLANES, N)


def gather_kernel(in_ref, *refs):
    phi_refs, orb_refs, table_ref, applied_refs, owner_refs = refs[:2], refs[2:4], refs[4], refs[5:7], refs[7:]

    @pl.when(pl.program_id(0) == 0)
    def _():
        for ref in applied_refs:
            ref[...] = jnp.zeros_like(ref)

    owners = [None, None]
    for pair in range(ORBS // 2):
        both = jnp.swapaxes(in_ref[:, 0, :, pair].reshape(N, 2 * PLANES, N), 0, 1)
        for j in (2 * pair, 2 * pair + 1):
            field = both[(j % 2) * PLANES:(j % 2 + 1) * PLANES].reshape(PLANES * N, N)
            field = turned(rows_by_table(field, table_ref[...]))
            result = (rows_by_table(field, table_ref[...]) * MIX).reshape(2, 2, N, N)
            for q in range(2):
                applied_refs[q][j] += result[q] * phi_refs[q][0]
                part = result[q] * orb_refs[q][j]
                owners[q] = part if j == 0 else owners[q] + part
    for ref, owner in zip(owner_refs, owners):
        ref[0] = owner


def params():
    return pltpu.CompilerParams(vmem_limit_bytes=VMEM)


def cost(planes):
    return pl.CostEstimate(flops=planes * N * N * 2048, bytes_accessed=planes * N * N * 12, transcendentals=0)


FIELD_SHAPE = jax.ShapeDtypeStruct((GROUP, SENT, LOCAL, ORBS // 2, 2 * PLANES, N), jnp.float32)
FIELD_BLOCK = pl.BlockSpec((GROUP, 1, LOCAL, ORBS // 2, 2 * PLANES, N), lambda i: (0, i, 0, 0, 0, 0))
SENT_BLOCK = pl.BlockSpec((1, 2, N, N), lambda i: (i, 0, 0, 0))
PLANE_SHAPE = jax.ShapeDtypeStruct((4, 2, N, N), jnp.float32)


def whole(array):
    return pl.BlockSpec(array.shape, lambda *_: (0,) * array.ndim)


def spread(phis, orbs, table):
    given = (*orbs, table)
    return pl.pallas_call(
        spread_kernel,
        grid=(SENT,),
        out_shape=FIELD_SHAPE,
        in_specs=[SENT_BLOCK] * 2 + [whole(array) for array in given],
        out_specs=FIELD_BLOCK,
        compiler_params=params(),
        cost_estimate=cost(SENT * ROWS),
    )(*phis, *given)


def lines(field, green, to_z, from_z):
    return pl.pallas_call(
        line_kernel,
        grid=(SENT,),
        out_shape=FIELD_SHAPE,
        in_specs=[FIELD_BLOCK, whole(green), whole(to_z), whole(from_z)],
        out_specs=FIELD_BLOCK,
        compiler_params=params(),
        cost_estimate=cost(SENT * ROWS),
    )(field, green, to_z, from_z)


def collect(field, phis, orbs, table):
    given = (*orbs, table)
    return pl.pallas_call(
        gather_kernel,
        grid=(SENT,),
        out_shape=(PLANE_SHAPE,) * 4,
        in_specs=[FIELD_BLOCK] + [SENT_BLOCK] * 2 + [whole(array) for array in given],
        out_specs=(whole(PLANE_SHAPE),) * 2 + (SENT_BLOCK,) * 2,
        compiler_params=params(),
        cost_estimate=cost(SENT * ROWS),
    )(field, *phis, *given)


def wavenumber(idx):
    shifted = jnp.where(idx < N // 2, idx, idx - N)
    return 2.0 * math.pi / (N * SPACING) * shifted.astype(jnp.float32)


def green_table(group):
    every = jnp.arange(N, dtype=jnp.int32)
    g_y = wavenumber(group * LOCAL + jnp.arange(LOCAL, dtype=jnp.int32))[:, None, None]
    g_z = wavenumber(every)[None, :, None]
    g_x = wavenumber(every)[None, None, :]
    ratio = (g_z * g_z + g_y * g_y + g_x * g_x) / (4.0 * OMEGA * OMEGA)
    safe = jnp.where(ratio > 0, ratio, 1.0)
    kernel = math.pi / (OMEGA * OMEGA) * jnp.where(ratio > 0, -jnp.expm1(-safe) / safe, 1.0)
    return kernel * (1.0 / N**3)


def over_core(array):
    return lax.ppermute(array, "fft", [(i, i ^ 1) for i in range(16)])


EVERY = ("band", "fft")
POOLS = [[4 * pool + k for k in range(4)] for pool in range(4)]
LINES = [[(4 * pool + k) * 16 + 2 * chip + c for chip in range(8) for k in range(4)] for pool in range(4) for c in range(2)]


def swap(array, axis, groups):
    return lax.all_to_all(array, axis, 0, 0, axis_index_groups=groups)


def to_pools(array, moves):
    return lax.ppermute(array, "band", [(4 * a + k, 4 * b + k) for a, b in moves for k in range(4)])


def around(array, distance):
    return to_pools(array, [(p, (p + distance) % 4) for p in range(4)])


def per_device(orbitals):
    place, band = lax.axis_index("fft"), lax.axis_index("band")
    core, pool = place % 2, band // 4
    table, to_z, from_z = (jnp.asarray(t) for t in cas_tables())
    to_z, from_z = (lax.dynamic_index_in_dim(t, core, 0, False) for t in (to_z, from_z))
    green = green_table(place // 2 * 4 + band % 4)

    held = swap(jnp.swapaxes(orbitals.reshape(2, 4, 2, N, N), 0, 1), "band", POOLS)
    near = held[0]
    across = to_pools(near, [(0, 2), (2, 0)])
    above = to_pools(near, [(0, 1), (2, 3)])
    below = to_pools(near, [(0, 3), (2, 1)])
    own = jnp.where(core == 0, held[:, 0], held[:, 1])
    orbs = (own, over_core(jnp.where(core == 0, held[:, 1], held[:, 0])))

    def pick(*options):
        return lax.select_n(pool, *options)

    phi = jnp.concatenate([pick(near, above, across, below), pick(across, below, near, above)])
    phis = (phi, over_core(phi))

    phis, orbs, green, to_z, from_z = lax.optimization_barrier((phis, orbs, green, to_z, from_z))
    field = swap(spread(phis, orbs, table), EVERY, LINES)
    field = swap(lines(field, green, to_z, from_z), EVERY, LINES)
    applied, applied_beside, owner, owner_beside = collect(field, phis, orbs, table)

    owner = owner + over_core(owner_beside)

    def part(distance):
        return lax.dynamic_index_in_dim(owner, lax.rem(pool + distance, 4), 0, False)

    share = part(0) + sum(around(part(d), d) for d in (1, 3, 2))
    shares = [share] + [around(share, d) for d in (1, 2, 3)]
    terms = jnp.stack([lax.select_n(pool, *(shares[(p - i) % 4] for p in range(4))) for i in range(SENT)])
    beside = over_core(applied_beside)
    back = jnp.stack([jnp.where(core == 0, applied, beside), jnp.where(core == 0, beside, applied)], 1)
    both = jnp.concatenate([back, jnp.broadcast_to(terms[None], (4,) + terms.shape)], 1)
    both = jnp.swapaxes(swap(both, "band", POOLS), 0, 1).reshape(6, SLAB, N, N)
    return both[:2], both[2:]


def solution(mesh):
    return jax.shard_map(
        per_device,
        mesh=mesh,
        in_specs=(P("band", "fft", None, None),),
        out_specs=(P("band", "fft", None, None), P(None, "fft", None, None)),
        check_vma=False,
    )
```

```python
import functools
import math

import jax
import jax.numpy as jnp
import ml_dtypes
import numpy as np
from jax import lax
from jax.experimental import pallas as pl
from jax.experimental.pallas import tpu as pltpu
from jax.sharding import PartitionSpec as P

N = 128
SPACING = 0.29
OMEGA = 0.106
MIX = -0.25
VMEM = 32 * 1024 * 1024
SLAB = 8
PLANES = 4
ORBS = 4
SENT = 4
GROUP = 32
LOCAL = N // GROUP
ROWS = ORBS * PLANES


def split(full):
    high = full.astype(ml_dtypes.bfloat16)
    low = (full - high.astype(np.float64)).astype(ml_dtypes.bfloat16)
    return np.concatenate([high, low], -1)


def cas_tables():
    idx = np.arange(N)
    angle = 2.0 * np.pi / N * (idx[:, None] * idx[None, :] % N)
    full = np.cos(angle) + np.sin(angle)
    to_z = np.zeros((2, 2 * N, 2, N))
    for c in range(2):
        held = [
            (j, (2 * chip + (c ^ q)) * SLAB + 2 * k + p)
            for chip in range(8) for k in range(4) for j in range(2) for q in range(2) for p in range(2)
        ]
        for row, (j, z) in enumerate(held):
            to_z[c, row, j] = full[z]
    to_z = to_z.reshape(2, 2 * N, 2 * N)
    pairs = [np.stack(np.split(split(t), 2, -1), 1) for t in (to_z, to_z.transpose(0, 2, 1))]
    return [np.concatenate([split(full)] * 2, 0)] + pairs


def halves(value):
    high = value.astype(jnp.bfloat16)
    low = (value - high.astype(jnp.float32)).astype(jnp.bfloat16)
    return high, low


def dot(a, b):
    return lax.dot_general(a, b, (((1,), (0,)), ((), ())), preferred_element_type=jnp.float32)


def rows_by_table(value, right):
    out = dot(jnp.concatenate(halves(value), 1), right)
    return out[:, :N] + out[:, N:]


def turned(value):
    return jnp.concatenate([value[r:r + N].T for r in range(0, value.shape[0], N)], 0)


def spread_kernel(phi_ref, phi_beside_ref, orb_ref, orb_beside_ref, table_ref, out_ref):
    @pl.loop(0, SENT)
    def _(i):
        fields = []
        for j in range(ORBS):
            density = [phi_ref[i, p] * orb_ref[j, p] for p in range(2)]
            density += [phi_beside_ref[i, p] * orb_beside_ref[j, p] for p in range(2)]
            field = turned(rows_by_table(jnp.concatenate(density, 0), table_ref[...]))
            fields.append(rows_by_table(field, table_ref[...]).reshape(PLANES, N, N))
        for j in range(0, ORBS, 2):
            pair = jnp.swapaxes(jnp.concatenate(fields[j:j + 2], 0), 0, 1)
            out_ref[:, i, :, j // 2] = pair.reshape(GROUP, LOCAL, 2 * PLANES, N)


def dot3(value, high, low):
    first, second = halves(value)
    return dot(first, high) + dot(second, high) + dot(first, low)


def line_kernel(in_ref, green_ref, to_z_ref, from_z_ref, out_ref):
    @pl.loop(0, SENT)
    def _(i):
        for a in range(LOCAL):
            green = jnp.concatenate([green_ref[a]] * 2, 1)
            for j in range(ORBS // 2):
                field = in_ref[:, i, a, j].reshape(2 * N, N)
                field = jnp.concatenate([field[:N].T, field[N:].T], 1)
                field = dot3(field, to_z_ref[0], to_z_ref[1]) * green
                field = dot3(field, from_z_ref[0], from_z_ref[1])
                field = jnp.concatenate([field[:, :N].T, field[:, N:].T], 0)
                out_ref[:, i, a, j] = field.reshape(GROUP, 2 * PLANES, N)


def gather_kernel(in_ref, *refs):
    phi_refs, orb_refs, table_ref, applied_refs, owner_refs = refs[:2], refs[2:4], refs[4], refs[5:7], refs[7:]
    for ref in applied_refs:
        ref[...] = jnp.zeros_like(ref)

    @pl.loop(0, SENT)
    def _(i):
        owners = [None, None]
        for pair in range(ORBS // 2):
            both = jnp.swapaxes(in_ref[:, i, :, pair].reshape(N, 2 * PLANES, N), 0, 1)
            for j in (2 * pair, 2 * pair + 1):
                field = both[(j % 2) * PLANES:(j % 2 + 1) * PLANES].reshape(PLANES * N, N)
                field = turned(rows_by_table(field, table_ref[...]))
                result = (rows_by_table(field, table_ref[...]) * MIX).reshape(2, 2, N, N)
                for q in range(2):
                    applied_refs[q][j] += result[q] * phi_refs[q][i]
                    part = result[q] * orb_refs[q][j]
                    owners[q] = part if j == 0 else owners[q] + part
        for ref, owner in zip(owner_refs, owners):
            ref[i] = owner


def params():
    return pltpu.CompilerParams(vmem_limit_bytes=VMEM)


def cost(planes):
    return pl.CostEstimate(flops=planes * N * N * 2048, bytes_accessed=planes * N * N * 12, transcendentals=0)


FIELD_SHAPE = jax.ShapeDtypeStruct((GROUP, SENT, LOCAL, ORBS // 2, 2 * PLANES, N), jnp.float32)
PLANE_SHAPE = jax.ShapeDtypeStruct((4, 2, N, N), jnp.float32)


def spread(phis, orbs, table):
    return pl.pallas_call(
        spread_kernel,
        out_shape=FIELD_SHAPE,
        compiler_params=params(),
        cost_estimate=cost(SENT * ROWS),
    )(*phis, *orbs, table)


def lines(field, green, to_z, from_z):
    return pl.pallas_call(
        line_kernel,
        out_shape=FIELD_SHAPE,
        compiler_params=params(),
        cost_estimate=cost(SENT * ROWS),
    )(field, green, to_z, from_z)


def collect(field, phis, orbs, table):
    return pl.pallas_call(
        gather_kernel,
        out_shape=(PLANE_SHAPE,) * 4,
        compiler_params=params(),
        cost_estimate=cost(SENT * ROWS),
    )(field, *phis, *orbs, table)


def wavenumber(idx):
    shifted = jnp.where(idx < N // 2, idx, idx - N)
    return 2.0 * math.pi / (N * SPACING) * shifted.astype(jnp.float32)


def green_table(group):
    every = jnp.arange(N, dtype=jnp.int32)
    g_y = wavenumber(group * LOCAL + jnp.arange(LOCAL, dtype=jnp.int32))[:, None, None]
    g_z = wavenumber(every)[None, :, None]
    g_x = wavenumber(every)[None, None, :]
    ratio = (g_z * g_z + g_y * g_y + g_x * g_x) / (4.0 * OMEGA * OMEGA)
    safe = jnp.where(ratio > 0, ratio, 1.0)
    kernel = math.pi / (OMEGA * OMEGA) * jnp.where(ratio > 0, -jnp.expm1(-safe) / safe, 1.0)
    return kernel * (1.0 / N**3)


def over_core(array):
    return lax.ppermute(array, "fft", [(i, i ^ 1) for i in range(16)])


EVERY = ("band", "fft")
POOLS = [[4 * pool + k for k in range(4)] for pool in range(4)]
LINES = [[(4 * pool + k) * 16 + 2 * chip + c for chip in range(8) for k in range(4)] for pool in range(4) for c in range(2)]


def swap(array, axis, groups):
    return lax.all_to_all(array, axis, 0, 0, axis_index_groups=groups)


def to_pools(array, moves):
    return lax.ppermute(array, "band", [(4 * a + k, 4 * b + k) for a, b in moves for k in range(4)])


def around(array, distance):
    return to_pools(array, [(p, (p + distance) % 4) for p in range(4)])


def per_device(orbitals):
    place, band = lax.axis_index("fft"), lax.axis_index("band")
    core, pool = place % 2, band // 4
    table, to_z, from_z = (jnp.asarray(t) for t in cas_tables())
    to_z, from_z = (lax.dynamic_index_in_dim(t, core, 0, False) for t in (to_z, from_z))
    green = green_table(place // 2 * 4 + band % 4)

    held = swap(jnp.swapaxes(orbitals.reshape(2, 4, 2, N, N), 0, 1), "band", POOLS)
    near = held[0]
    across = to_pools(near, [(0, 2), (2, 0)])
    above = to_pools(near, [(0, 1), (2, 3)])
    below = to_pools(near, [(0, 3), (2, 1)])
    own = jnp.where(core == 0, held[:, 0], held[:, 1])
    orbs = (own, over_core(jnp.where(core == 0, held[:, 1], held[:, 0])))

    def pick(*options):
        return lax.select_n(pool, *options)

    phi = jnp.concatenate([pick(near, above, across, below), pick(across, below, near, above)])
    phis = (phi, over_core(phi))

    phis, orbs, green, to_z, from_z = lax.optimization_barrier((phis, orbs, green, to_z, from_z))
    field = swap(spread(phis, orbs, table), EVERY, LINES)
    field = swap(lines(field, green, to_z, from_z), EVERY, LINES)
    applied, applied_beside, owner, owner_beside = collect(field, phis, orbs, table)

    owner = owner + over_core(owner_beside)

    def part(distance):
        return lax.dynamic_index_in_dim(owner, lax.rem(pool + distance, 4), 0, False)

    share = part(0) + sum(around(part(d), d) for d in (1, 3, 2))
    shares = [share] + [around(share, d) for d in (1, 2, 3)]
    terms = jnp.stack([lax.select_n(pool, *(shares[(p - i) % 4] for p in range(4))) for i in range(SENT)])
    beside = over_core(applied_beside)
    back = jnp.stack([jnp.where(core == 0, applied, beside), jnp.where(core == 0, beside, applied)], 1)
    both = jnp.concatenate([back, jnp.broadcast_to(terms[None], (4,) + terms.shape)], 1)
    both = jnp.swapaxes(swap(both, "band", POOLS), 0, 1).reshape(6, SLAB, N, N)
    return both[:2], both[2:]


def solution(mesh):
    return jax.shard_map(
        per_device,
        mesh=mesh,
        in_specs=(P("band", "fft", None, None),),
        out_specs=(P("band", "fft", None, None), P(None, "fft", None, None)),
        check_vma=False,
    )
```

```python
import functools
import math

import jax
import jax.numpy as jnp
import ml_dtypes
import numpy as np
from jax import lax
from jax.experimental import pallas as pl
from jax.experimental.pallas import tpu as pltpu
from jax.sharding import PartitionSpec as P

N = 128
SPACING = 0.29
OMEGA = 0.106
MIX = -0.25
VMEM = 32 * 1024 * 1024
SLAB = 8
PLANES = 4
ORBS = 4
SENT = 4
GROUP = 32
LOCAL = N // GROUP
ROWS = ORBS * PLANES
PLACES = [(4 * y_lo + x, 2 * z + y_hi) for y_hi in range(2) for y_lo in range(2) for x in range(4) for z in range(2)]


def split(full):
    high = full.astype(ml_dtypes.bfloat16)
    low = (full - high.astype(np.float64)).astype(ml_dtypes.bfloat16)
    return np.concatenate([high, low], -1)


def cas_tables():
    idx = np.arange(N)
    angle = 2.0 * np.pi / N * (idx[:, None] * idx[None, :] % N)
    full = np.cos(angle) + np.sin(angle)
    to_z = np.zeros((2, 2 * N, 2, N))
    for c in range(2):
        held = [
            (j, (2 * chip + (c ^ q)) * SLAB + 2 * k + p)
            for chip, k in PLACES for j in range(2) for q in range(2) for p in range(2)
        ]
        for row, (j, z) in enumerate(held):
            to_z[c, row, j] = full[z]
    to_z = to_z.reshape(2, 2 * N, 2 * N)
    pairs = [np.stack(np.split(split(t), 2, -1), 1) for t in (to_z, to_z.transpose(0, 2, 1))]
    return [np.concatenate([split(full)] * 2, 0)] + pairs


def halves(value):
    high = value.astype(jnp.bfloat16)
    low = (value - high.astype(jnp.float32)).astype(jnp.bfloat16)
    return high, low


def dot(a, b):
    return lax.dot_general(a, b, (((1,), (0,)), ((), ())), preferred_element_type=jnp.float32)


def rows_by_table(value, right):
    out = dot(jnp.concatenate(halves(value), 1), right)
    return out[:, :N] + out[:, N:]


def turned(value):
    return jnp.concatenate([value[r:r + N].T for r in range(0, value.shape[0], N)], 0)


def spread_kernel(phi_ref, phi_beside_ref, orb_ref, orb_beside_ref, table_ref, out_ref):
    @pl.loop(0, SENT)
    def _(i):
        fields = []
        for j in range(ORBS):
            density = [phi_ref[i, p] * orb_ref[j, p] for p in range(2)]
            density += [phi_beside_ref[i, p] * orb_beside_ref[j, p] for p in range(2)]
            field = turned(rows_by_table(jnp.concatenate(density, 0), table_ref[...]))
            fields.append(rows_by_table(field, table_ref[...]).reshape(PLANES, N, N))
        for j in range(0, ORBS, 2):
            pair = jnp.swapaxes(jnp.concatenate(fields[j:j + 2], 0), 0, 1)
            out_ref[:, i, :, j // 2] = pair.reshape(GROUP, LOCAL, 2 * PLANES, N)


def dot3(value, high, low):
    first, second = halves(value)
    return dot(first, high) + dot(second, high) + dot(first, low)


def line_kernel(in_ref, green_ref, to_z_ref, from_z_ref, out_ref):
    @pl.loop(0, SENT)
    def _(i):
        for a in range(LOCAL):
            green = jnp.concatenate([green_ref[a]] * 2, 1)
            for j in range(ORBS // 2):
                field = in_ref[:, i, a, j].reshape(2 * N, N)
                field = jnp.concatenate([field[:N].T, field[N:].T], 1)
                field = dot3(field, to_z_ref[0], to_z_ref[1]) * green
                field = dot3(field, from_z_ref[0], from_z_ref[1])
                field = jnp.concatenate([field[:, :N].T, field[:, N:].T], 0)
                out_ref[:, i, a, j] = field.reshape(GROUP, 2 * PLANES, N)


def gather_kernel(in_ref, *refs):
    phi_refs, orb_refs, table_ref, applied_refs, owner_refs = refs[:2], refs[2:4], refs[4], refs[5:7], refs[7:]
    for ref in applied_refs:
        ref[...] = jnp.zeros_like(ref)

    @pl.loop(0, SENT)
    def _(i):
        owners = [None, None]
        for pair in range(ORBS // 2):
            both = jnp.swapaxes(in_ref[:, i, :, pair].reshape(N, 2 * PLANES, N), 0, 1)
            for j in (2 * pair, 2 * pair + 1):
                field = both[(j % 2) * PLANES:(j % 2 + 1) * PLANES].reshape(PLANES * N, N)
                field = turned(rows_by_table(field, table_ref[...]))
                result = (rows_by_table(field, table_ref[...]) * MIX).reshape(2, 2, N, N)
                for q in range(2):
                    applied_refs[q][j] += result[q] * phi_refs[q][i]
                    part = result[q] * orb_refs[q][j]
                    owners[q] = part if j == 0 else owners[q] + part
        for ref, owner in zip(owner_refs, owners):
            ref[i] = owner


def join_kernel(in_ref, applied_ref, terms_ref, sems):
    refs = [applied_ref.at[i] for i in range(2)] + [terms_ref.at[i] for i in range(SENT)]
    pairs = [(in_ref.at[k, i], ref.at[pl.ds(2 * k, 2)]) for k in range(4) for i, ref in enumerate(refs)]
    copies = [pltpu.make_async_copy(source, target, sems.at[n]) for n, (source, target) in enumerate(pairs)]
    for copy in copies:
        copy.start()
    for copy in copies:
        copy.wait()


def params():
    return pltpu.CompilerParams(vmem_limit_bytes=VMEM)


def cost(planes):
    return pl.CostEstimate(flops=planes * N * N * 2048, bytes_accessed=planes * N * N * 12, transcendentals=0)


FIELD_SHAPE = jax.ShapeDtypeStruct((GROUP, SENT, LOCAL, ORBS // 2, 2 * PLANES, N), jnp.float32)
PLANE_SHAPE = jax.ShapeDtypeStruct((4, 2, N, N), jnp.float32)


def spread(phis, orbs, table):
    return pl.pallas_call(
        spread_kernel,
        out_shape=FIELD_SHAPE,
        compiler_params=params(),
        cost_estimate=cost(SENT * ROWS),
    )(*phis, *orbs, table)


def lines(field, green, to_z, from_z):
    return pl.pallas_call(
        line_kernel,
        out_shape=FIELD_SHAPE,
        compiler_params=params(),
        cost_estimate=cost(SENT * ROWS),
    )(field, green, to_z, from_z)


def collect(field, phis, orbs, table):
    return pl.pallas_call(
        gather_kernel,
        out_shape=(PLANE_SHAPE,) * 4,
        compiler_params=params(),
        cost_estimate=cost(SENT * ROWS),
    )(field, *phis, *orbs, table)


def join(both):
    return pl.pallas_call(
        join_kernel,
        out_shape=tuple(jax.ShapeDtypeStruct((n, SLAB, N, N), jnp.float32) for n in (2, SENT)),
        in_specs=[pl.BlockSpec(memory_space=pltpu.VMEM)],
        out_specs=(pl.BlockSpec(memory_space=pl.ANY),) * 2,
        scratch_shapes=[pltpu.SemaphoreType.DMA((24,))],
        compiler_params=params(),
    )(both)


def wavenumber(idx):
    shifted = jnp.where(idx < N // 2, idx, idx - N)
    return 2.0 * math.pi / (N * SPACING) * shifted.astype(jnp.float32)


def green_table(group):
    every = jnp.arange(N, dtype=jnp.int32)
    g_y = wavenumber(group * LOCAL + jnp.arange(LOCAL, dtype=jnp.int32))[:, None, None]
    g_z = wavenumber(every)[None, :, None]
    g_x = wavenumber(every)[None, None, :]
    ratio = (g_z * g_z + g_y * g_y + g_x * g_x) / (4.0 * OMEGA * OMEGA)
    safe = jnp.where(ratio > 0, ratio, 1.0)
    kernel = math.pi / (OMEGA * OMEGA) * jnp.where(ratio > 0, -jnp.expm1(-safe) / safe, 1.0)
    return kernel * (1.0 / N**3)


def over_core(array):
    return lax.ppermute(array, "fft", [(i, i ^ 1) for i in range(16)])


EVERY = ("band", "fft")
POOLS = [[4 * pool + k for k in range(4)] for pool in range(4)]
LINES = [[(4 * pool + k) * 16 + 2 * chip + c for chip, k in PLACES] for pool in range(4) for c in range(2)]


def swap(array, axis, groups):
    return lax.all_to_all(array, axis, 0, 0, axis_index_groups=groups)


def to_pools(array, moves):
    return lax.ppermute(array, "band", [(4 * a + k, 4 * b + k) for a, b in moves for k in range(4)])


def around(array, distance):
    return to_pools(array, [(p, (p + distance) % 4) for p in range(4)])


def per_device(orbitals):
    place, band = lax.axis_index("fft"), lax.axis_index("band")
    core, pool = place % 2, band // 4
    table, to_z, from_z = (jnp.asarray(t) for t in cas_tables())
    to_z, from_z = (lax.dynamic_index_in_dim(t, core, 0, False) for t in (to_z, from_z))
    green = green_table(band % 2 * 16 + place // 2 * 2 + band // 2 % 2)

    held = swap(jnp.swapaxes(orbitals.reshape(2, 4, 2, N, N), 0, 1), "band", POOLS)
    near = held[0]
    across = to_pools(near, [(0, 2), (2, 0)])
    above = to_pools(near, [(0, 1), (2, 3)])
    below = to_pools(near, [(0, 3), (2, 1)])
    own = jnp.where(core == 0, held[:, 0], held[:, 1])
    orbs = (own, over_core(jnp.where(core == 0, held[:, 1], held[:, 0])))

    def pick(*options):
        return lax.select_n(pool, *options)

    phi = jnp.concatenate([pick(near, above, across, below), pick(across, below, near, above)])
    phis = (phi, over_core(phi))

    phis, orbs, green, to_z, from_z = lax.optimization_barrier((phis, orbs, green, to_z, from_z))
    field = swap(spread(phis, orbs, table), EVERY, LINES)
    field = swap(lines(field, green, to_z, from_z), EVERY, LINES)
    applied, applied_beside, owner, owner_beside = collect(field, phis, orbs, table)

    owner = owner + over_core(owner_beside)

    def part(distance):
        return lax.dynamic_index_in_dim(owner, lax.rem(pool + distance, 4), 0, False)

    share = part(0) + sum(around(part(d), d) for d in (1, 3, 2))
    shares = [share] + [around(share, d) for d in (1, 2, 3)]
    terms = jnp.stack([lax.select_n(pool, *(shares[(p - i) % 4] for p in range(4))) for i in range(SENT)])
    beside = over_core(applied_beside)
    back = jnp.stack([jnp.where(core == 0, applied, beside), jnp.where(core == 0, beside, applied)], 1)
    both = jnp.concatenate([back, jnp.broadcast_to(terms[None], (4,) + terms.shape)], 1)
    return join(swap(both, "band", POOLS))


def solution(mesh):
    return jax.shard_map(
        per_device,
        mesh=mesh,
        in_specs=(P("band", "fft", None, None),),
        out_specs=(P("band", "fft", None, None), P(None, "fft", None, None)),
        check_vma=False,
    )
```

```python
import functools
import math

import jax
import jax.numpy as jnp
import ml_dtypes
import numpy as np
from jax import lax
from jax.experimental import pallas as pl
from jax.experimental.pallas import tpu as pltpu
from jax.sharding import PartitionSpec as P

N = 128
SPACING = 0.29
OMEGA = 0.106
MIX = -0.25
VMEM = 32 * 1024 * 1024
SLAB = 8
PLANES = 4
ORBS = 4
SENT = 4
GROUP = 32
LOCAL = N // GROUP
ROWS = ORBS * PLANES
PLACES = [(4 * y_lo + x, 2 * z + y_hi) for y_hi in range(2) for y_lo in range(2) for x in range(4) for z in range(2)]


def split(full):
    high = full.astype(ml_dtypes.bfloat16)
    low = (full - high.astype(np.float64)).astype(ml_dtypes.bfloat16)
    return np.concatenate([high, low], -1)


def cas_tables():
    idx = np.arange(N)
    angle = 2.0 * np.pi / N * (idx[:, None] * idx[None, :] % N)
    full = np.cos(angle) + np.sin(angle)
    to_z = np.zeros((2, 2 * N, 2, N))
    for c in range(2):
        held = [
            (j, (2 * chip + (c ^ q)) * SLAB + 2 * k + p)
            for chip, k in PLACES for j in range(2) for q in range(2) for p in range(2)
        ]
        for row, (j, z) in enumerate(held):
            to_z[c, row, j] = full[z]
    to_z = to_z.reshape(2, 2 * N, 2 * N)
    pairs = [np.stack(np.split(split(t), 2, -1), 1) for t in (to_z, to_z.transpose(0, 2, 1))]
    return [np.concatenate([split(full)] * 2, 0)] + pairs


def halves(value):
    high = value.astype(jnp.bfloat16)
    low = (value - high.astype(jnp.float32)).astype(jnp.bfloat16)
    return high, low


def dot(a, b):
    return lax.dot_general(a, b, (((1,), (0,)), ((), ())), preferred_element_type=jnp.float32)


def rows_by_table(value, right):
    out = dot(jnp.concatenate(halves(value), 1), right)
    return out[:, :N] + out[:, N:]


def turned(value):
    return jnp.concatenate([value[r:r + N].T for r in range(0, value.shape[0], N)], 0)


def spread_kernel(phi_ref, phi_beside_ref, orb_ref, orb_beside_ref, table_ref, out_ref):
    @pl.loop(0, SENT)
    def _(i):
        fields = []
        for j in range(ORBS):
            density = [phi_ref[i, p] * orb_ref[j, p] for p in range(2)]
            density += [phi_beside_ref[i, p] * orb_beside_ref[j, p] for p in range(2)]
            field = turned(rows_by_table(jnp.concatenate(density, 0), table_ref[...]))
            fields.append(rows_by_table(field, table_ref[...]).reshape(PLANES, N, N))
        for j in range(0, ORBS, 2):
            pair = jnp.swapaxes(jnp.concatenate(fields[j:j + 2], 0), 0, 1)
            out_ref[:, i, :, j // 2] = pair.reshape(GROUP, LOCAL, 2 * PLANES, N)


def dot3(value, high, low):
    first, second = halves(value)
    return dot(first, high) + dot(second, high) + dot(first, low)


def line_kernel(in_ref, green_ref, to_z_ref, from_z_ref, out_ref):
    @pl.loop(0, SENT)
    def _(i):
        for a in range(LOCAL):
            green = jnp.concatenate([green_ref[a]] * 2, 1)
            for j in range(ORBS // 2):
                field = in_ref[:, i, a, j].reshape(2 * N, N)
                field = jnp.concatenate([field[:N].T, field[N:].T], 1)
                field = dot3(field, to_z_ref[0], to_z_ref[1]) * green
                field = dot3(field, from_z_ref[0], from_z_ref[1])
                field = jnp.concatenate([field[:, :N].T, field[:, N:].T], 0)
                out_ref[:, i, a, j] = field.reshape(GROUP, 2 * PLANES, N)


def gather_kernel(in_ref, *refs):
    phi_refs, orb_refs, table_ref, applied_refs, owner_refs = refs[:2], refs[2:4], refs[4], refs[5:7], refs[7:]
    for ref in applied_refs:
        ref[...] = jnp.zeros_like(ref)

    @pl.loop(0, SENT)
    def _(i):
        owners = [None, None]
        for pair in range(ORBS // 2):
            both = jnp.swapaxes(in_ref[:, i, :, pair].reshape(N, 2 * PLANES, N), 0, 1)
            for j in (2 * pair, 2 * pair + 1):
                field = both[(j % 2) * PLANES:(j % 2 + 1) * PLANES].reshape(PLANES * N, N)
                field = turned(rows_by_table(field, table_ref[...]))
                result = (rows_by_table(field, table_ref[...]) * MIX).reshape(2, 2, N, N)
                for q in range(2):
                    applied_refs[q][j] += result[q] * phi_refs[q][i]
                    part = result[q] * orb_refs[q][j]
                    owners[q] = part if j == 0 else owners[q] + part
        for ref, owner in zip(owner_refs, owners):
            ref[i] = owner


def join_kernel(in_ref, applied_ref, terms_ref, sems):
    refs = [applied_ref.at[i] for i in range(2)] + [terms_ref.at[i] for i in range(SENT)]
    pairs = [(in_ref.at[k, i], ref.at[pl.ds(2 * k, 2)]) for k in range(4) for i, ref in enumerate(refs)]
    copies = [pltpu.make_async_copy(source, target, sems.at[n]) for n, (source, target) in enumerate(pairs)]
    for copy in copies:
        copy.start()
    for copy in copies:
        copy.wait()


def params():
    return pltpu.CompilerParams(vmem_limit_bytes=VMEM)


def cost(planes):
    return pl.CostEstimate(flops=planes * N * N * 2048, bytes_accessed=planes * N * N * 12, transcendentals=0)


FIELD_SHAPE = jax.ShapeDtypeStruct((GROUP, SENT, LOCAL, ORBS // 2, 2 * PLANES, N), jnp.float32)
PLANE_SHAPE = jax.ShapeDtypeStruct((4, 2, N, N), jnp.float32)


def spread(phis, orbs, table):
    return pl.pallas_call(
        spread_kernel,
        out_shape=FIELD_SHAPE,
        compiler_params=params(),
        cost_estimate=cost(SENT * ROWS),
    )(*phis, *orbs, table)


def lines(field, green, to_z, from_z):
    return pl.pallas_call(
        line_kernel,
        out_shape=FIELD_SHAPE,
        compiler_params=params(),
        cost_estimate=cost(SENT * ROWS),
    )(field, green, to_z, from_z)


def collect(field, phis, orbs, table):
    return pl.pallas_call(
        gather_kernel,
        out_shape=(PLANE_SHAPE,) * 4,
        compiler_params=params(),
        cost_estimate=cost(SENT * ROWS),
    )(field, *phis, *orbs, table)


def join(both):
    return pl.pallas_call(
        join_kernel,
        out_shape=tuple(jax.ShapeDtypeStruct((n, SLAB, N, N), jnp.float32) for n in (2, SENT)),
        in_specs=[pl.BlockSpec(memory_space=pltpu.VMEM)],
        out_specs=(pl.BlockSpec(memory_space=pl.ANY),) * 2,
        scratch_shapes=[pltpu.SemaphoreType.DMA((24,))],
        compiler_params=params(),
    )(both)


def wavenumber(idx):
    shifted = jnp.where(idx < N // 2, idx, idx - N)
    return 2.0 * math.pi / (N * SPACING) * shifted.astype(jnp.float32)


def green_table(group):
    every = jnp.arange(N, dtype=jnp.int32)
    g_y = wavenumber(group * LOCAL + jnp.arange(LOCAL, dtype=jnp.int32))[:, None, None]
    g_z = wavenumber(every)[None, :, None]
    g_x = wavenumber(every)[None, None, :]
    ratio = (g_z * g_z + g_y * g_y + g_x * g_x) / (4.0 * OMEGA * OMEGA)
    safe = jnp.where(ratio > 0, ratio, 1.0)
    kernel = math.pi / (OMEGA * OMEGA) * jnp.where(ratio > 0, -jnp.expm1(-safe) / safe, 1.0)
    return kernel * (1.0 / N**3)


def over_core(array):
    return lax.ppermute(array, "fft", [(i, i ^ 1) for i in range(16)])


EVERY = ("band", "fft")
POOLS = [[4 * pool + k for k in range(4)] for pool in range(4)]
LINES = [[(4 * pool + k) * 16 + 2 * chip + c for chip, k in PLACES] for pool in range(4) for c in range(2)]


def swap(array, axis, groups):
    return lax.all_to_all(array, axis, 0, 0, axis_index_groups=groups)


def to_pools(array, moves):
    return lax.ppermute(array, "band", [(4 * a + k, 4 * b + k) for a, b in moves for k in range(4)])


def around(array, distance):
    return to_pools(array, [(p, (p + distance) % 4) for p in range(4)])


def per_device(orbitals):
    place, band = lax.axis_index("fft"), lax.axis_index("band")
    core, pool = place % 2, band // 4
    table, to_z, from_z = (jnp.asarray(t) for t in cas_tables())
    to_z, from_z = (lax.dynamic_index_in_dim(t, core, 0, False) for t in (to_z, from_z))
    green = green_table(band % 2 * 16 + place // 2 * 2 + band // 2 % 2)

    held = swap(jnp.swapaxes(orbitals.reshape(2, 4, 2, N, N), 0, 1), "band", POOLS)
    near = held[0]
    across = to_pools(near, [(0, 2), (2, 0)])
    above = to_pools(near, [(0, 1), (2, 3)])
    below = to_pools(near, [(0, 3), (2, 1)])
    own = jnp.where(core == 0, held[:, 0], held[:, 1])
    orbs = (own, over_core(jnp.where(core == 0, held[:, 1], held[:, 0])))

    def pick(*options):
        return lax.select_n(pool, *options)

    phi = jnp.concatenate([pick(near, above, across, below), pick(across, below, near, above)])
    phis = (phi, over_core(phi))

    phis, orbs, green, to_z, from_z = lax.optimization_barrier((phis, orbs, green, to_z, from_z))
    field = swap(spread(phis, orbs, table), EVERY, LINES)
    field = swap(lines(field, green, to_z, from_z), EVERY, LINES)
    applied, applied_beside, owner, owner_beside = collect(field, phis, orbs, table)

    owner = owner + over_core(owner_beside)

    def part(distance):
        return lax.dynamic_index_in_dim(owner, lax.rem(pool + distance, 4), 0, False)

    share = part(0) + sum(around(part(d), d) for d in (2, 1, 3))
    shares = {0: share, **{d: around(share, d) for d in (2, 1, 3)}}
    terms = jnp.stack([lax.select_n(pool, *(shares[(p - i) % 4] for p in range(4))) for i in range(SENT)])
    beside = over_core(applied_beside)
    back = jnp.stack([jnp.where(core == 0, applied, beside), jnp.where(core == 0, beside, applied)], 1)
    both = jnp.concatenate([back, jnp.broadcast_to(terms[None], (4,) + terms.shape)], 1)
    return join(swap(both, "band", POOLS))


def solution(mesh):
    return jax.shard_map(
        per_device,
        mesh=mesh,
        in_specs=(P("band", "fft", None, None),),
        out_specs=(P("band", "fft", None, None), P(None, "fft", None, None)),
        check_vma=False,
    )
```

```python
import functools
import math

import jax
import jax.numpy as jnp
import ml_dtypes
import numpy as np
from jax import lax
from jax.experimental import pallas as pl
from jax.experimental.pallas import tpu as pltpu
from jax.sharding import PartitionSpec as P

N = 128
SPACING = 0.29
OMEGA = 0.106
MIX = -0.25
VMEM = 32 * 1024 * 1024
SLAB = 8
PLANES = 4
ORBS = 4
SENT = 4
GROUP = 32
LOCAL = N // GROUP
ROWS = ORBS * PLANES
PLACES = [(4 * y_lo + x, 2 * z + y_hi) for y_hi in range(2) for y_lo in range(2) for x in range(4) for z in range(2)]


def split(full):
    high = full.astype(ml_dtypes.bfloat16)
    low = (full - high.astype(np.float64)).astype(ml_dtypes.bfloat16)
    return np.concatenate([high, low], -1)


def cas_tables():
    idx = np.arange(N)
    angle = 2.0 * np.pi / N * (idx[:, None] * idx[None, :] % N)
    full = np.cos(angle) + np.sin(angle)
    to_z = np.zeros((2, 2 * N, 2, N))
    for c in range(2):
        held = [
            (j, (2 * chip + (c ^ q)) * SLAB + 2 * k + p)
            for chip, k in PLACES for j in range(2) for q in range(2) for p in range(2)
        ]
        for row, (j, z) in enumerate(held):
            to_z[c, row, j] = full[z]
    to_z = to_z.reshape(2, 2 * N, 2 * N)
    pairs = [np.stack(np.split(split(t), 2, -1), 1) for t in (to_z, to_z.transpose(0, 2, 1))]
    return [np.concatenate([split(full)] * 2, 0)] + pairs


def halves(value):
    high = value.astype(jnp.bfloat16)
    low = (value - high.astype(jnp.float32)).astype(jnp.bfloat16)
    return high, low


def dot(a, b):
    return lax.dot_general(a, b, (((1,), (0,)), ((), ())), preferred_element_type=jnp.float32)


def rows_by_table(value, right):
    out = dot(jnp.concatenate(halves(value), 1), right)
    return out[:, :N] + out[:, N:]


def turned(value):
    return jnp.concatenate([value[r:r + N].T for r in range(0, value.shape[0], N)], 0)


def spread_kernel(phi_ref, phi_beside_ref, orb_ref, orb_beside_ref, table_ref, out_ref):
    @pl.loop(0, SENT)
    def _(i):
        fields = []
        for j in range(ORBS):
            density = [phi_ref[i, p] * orb_ref[j, p] for p in range(2)]
            density += [phi_beside_ref[i, p] * orb_beside_ref[j, p] for p in range(2)]
            field = turned(rows_by_table(jnp.concatenate(density, 0), table_ref[...]))
            fields.append(rows_by_table(field, table_ref[...]).reshape(PLANES, N, N))
        for j in range(0, ORBS, 2):
            pair = jnp.swapaxes(jnp.concatenate(fields[j:j + 2], 0), 0, 1)
            out_ref[:, i, :, j // 2] = pair.reshape(GROUP, LOCAL, 2 * PLANES, N)


def dot3(value, high, low):
    first, second = halves(value)
    return dot(first, high) + dot(second, high) + dot(first, low)


def line_kernel(in_ref, green_ref, to_z_ref, from_z_ref, out_ref):
    @pl.loop(0, SENT)
    def _(i):
        for a in range(LOCAL):
            green = jnp.concatenate([green_ref[a]] * 2, 1)
            for j in range(ORBS // 2):
                field = in_ref[:, i, a, j].reshape(2 * N, N)
                field = jnp.concatenate([field[:N].T, field[N:].T], 1)
                field = dot3(field, to_z_ref[0], to_z_ref[1]) * green
                field = dot3(field, from_z_ref[0], from_z_ref[1])
                field = jnp.concatenate([field[:, :N].T, field[:, N:].T], 0)
                out_ref[:, i, a, j] = field.reshape(GROUP, 2 * PLANES, N)


def gather_kernel(side, in_ref, phi_ref, orb_ref, table_ref, applied_ref, owner_ref):
    applied_ref[...] = jnp.zeros_like(applied_ref)

    @pl.loop(0, SENT)
    def _(i):
        owner = None
        for pair in range(ORBS // 2):
            both = jnp.swapaxes(in_ref[:, i, :, pair].reshape(N, 2 * PLANES, N), 0, 1)
            first = 2 * side
            field = jnp.concatenate([both[first:first + 2], both[PLANES + first:PLANES + first + 2]], 0)
            field = turned(rows_by_table(field.reshape(PLANES * N, N), table_ref[...]))
            result = (rows_by_table(field, table_ref[...]) * MIX).reshape(2, 2, N, N)
            for n in range(2):
                j = 2 * pair + n
                applied_ref[j] += result[n] * phi_ref[i]
                part = result[n] * orb_ref[j]
                owner = part if j == 0 else owner + part
        owner_ref[i] = owner


def join_kernel(in_ref, applied_ref, terms_ref, sems):
    refs = [applied_ref.at[i] for i in range(2)] + [terms_ref.at[i] for i in range(SENT)]
    pairs = [(in_ref.at[k, i], ref.at[pl.ds(2 * k, 2)]) for k in range(4) for i, ref in enumerate(refs)]
    copies = [pltpu.make_async_copy(source, target, sems.at[n]) for n, (source, target) in enumerate(pairs)]
    for copy in copies:
        copy.start()
    for copy in copies:
        copy.wait()


def params():
    return pltpu.CompilerParams(vmem_limit_bytes=VMEM)


def cost(planes):
    return pl.CostEstimate(flops=planes * N * N * 2048, bytes_accessed=planes * N * N * 12, transcendentals=0)


FIELD_SHAPE = jax.ShapeDtypeStruct((GROUP, SENT, LOCAL, ORBS // 2, 2 * PLANES, N), jnp.float32)
PLANE_SHAPE = jax.ShapeDtypeStruct((4, 2, N, N), jnp.float32)


def spread(phis, orbs, table):
    return pl.pallas_call(
        spread_kernel,
        out_shape=FIELD_SHAPE,
        compiler_params=params(),
        cost_estimate=cost(SENT * ROWS),
    )(*phis, *orbs, table)


def lines(field, green, to_z, from_z):
    return pl.pallas_call(
        line_kernel,
        out_shape=FIELD_SHAPE,
        compiler_params=params(),
        cost_estimate=cost(SENT * ROWS),
    )(field, green, to_z, from_z)


def collect(side, field, phis, orbs, table):
    return pl.pallas_call(
        functools.partial(gather_kernel, side),
        out_shape=(PLANE_SHAPE,) * 2,
        compiler_params=params(),
        cost_estimate=cost(SENT * ROWS // 2),
    )(field, phis[side], orbs[side], table)


def join(both):
    return pl.pallas_call(
        join_kernel,
        out_shape=tuple(jax.ShapeDtypeStruct((n, SLAB, N, N), jnp.float32) for n in (2, SENT)),
        in_specs=[pl.BlockSpec(memory_space=pltpu.VMEM)],
        out_specs=(pl.BlockSpec(memory_space=pl.ANY),) * 2,
        scratch_shapes=[pltpu.SemaphoreType.DMA((24,))],
        compiler_params=params(),
    )(both)


def wavenumber(idx):
    shifted = jnp.where(idx < N // 2, idx, idx - N)
    return 2.0 * math.pi / (N * SPACING) * shifted.astype(jnp.float32)


def green_table(group):
    every = jnp.arange(N, dtype=jnp.int32)
    g_y = wavenumber(group * LOCAL + jnp.arange(LOCAL, dtype=jnp.int32))[:, None, None]
    g_z = wavenumber(every)[None, :, None]
    g_x = wavenumber(every)[None, None, :]
    ratio = (g_z * g_z + g_y * g_y + g_x * g_x) / (4.0 * OMEGA * OMEGA)
    safe = jnp.where(ratio > 0, ratio, 1.0)
    kernel = math.pi / (OMEGA * OMEGA) * jnp.where(ratio > 0, -jnp.expm1(-safe) / safe, 1.0)
    return kernel * (1.0 / N**3)


def over_core(array):
    return lax.ppermute(array, "fft", [(i, i ^ 1) for i in range(16)])


EVERY = ("band", "fft")
POOLS = [[4 * pool + k for k in range(4)] for pool in range(4)]
LINES = [[(4 * pool + k) * 16 + 2 * chip + c for chip, k in PLACES] for pool in range(4) for c in range(2)]


def swap(array, axis, groups):
    return lax.all_to_all(array, axis, 0, 0, axis_index_groups=groups)


def to_pools(array, moves):
    return lax.ppermute(array, "band", [(4 * a + k, 4 * b + k) for a, b in moves for k in range(4)])


def around(array, distance):
    return to_pools(array, [(p, (p + distance) % 4) for p in range(4)])


def per_device(orbitals):
    place, band = lax.axis_index("fft"), lax.axis_index("band")
    core, pool = place % 2, band // 4
    table, to_z, from_z = (jnp.asarray(t) for t in cas_tables())
    to_z, from_z = (lax.dynamic_index_in_dim(t, core, 0, False) for t in (to_z, from_z))
    green = green_table(band % 2 * 16 + place // 2 * 2 + band // 2 % 2)

    held = swap(jnp.swapaxes(orbitals.reshape(2, 4, 2, N, N), 0, 1), "band", POOLS)
    near = held[0]
    across = to_pools(near, [(0, 2), (2, 0)])
    above = to_pools(near, [(0, 1), (2, 3)])
    below = to_pools(near, [(0, 3), (2, 1)])
    own = jnp.where(core == 0, held[:, 0], held[:, 1])
    orbs = (own, over_core(jnp.where(core == 0, held[:, 1], held[:, 0])))

    def pick(*options):
        return lax.select_n(pool, *options)

    phi = jnp.concatenate([pick(near, above, across, below), pick(across, below, near, above)])
    phis = (phi, over_core(phi))

    phis, orbs, green, to_z, from_z = lax.optimization_barrier((phis, orbs, green, to_z, from_z))
    field = swap(spread(phis, orbs, table), EVERY, LINES)
    field = swap(lines(field, green, to_z, from_z), EVERY, LINES)
    applied_beside, owner_beside = collect(1, field, phis, orbs, table)
    applied, owner = collect(0, field, phis, orbs, table)

    owner = owner + over_core(owner_beside)

    def part(distance):
        return lax.dynamic_index_in_dim(owner, lax.rem(pool + distance, 4), 0, False)

    share = part(0) + sum(around(part(d), d) for d in (1, 3, 2))
    shares = [share] + [around(share, d) for d in (1, 2, 3)]
    terms = jnp.stack([lax.select_n(pool, *(shares[(p - i) % 4] for p in range(4))) for i in range(SENT)])
    beside = over_core(applied_beside)
    back = jnp.stack([jnp.where(core == 0, applied, beside), jnp.where(core == 0, beside, applied)], 1)
    both = jnp.concatenate([back, jnp.broadcast_to(terms[None], (4,) + terms.shape)], 1)
    return join(swap(both, "band", POOLS))


def solution(mesh):
    return jax.shard_map(
        per_device,
        mesh=mesh,
        in_specs=(P("band", "fft", None, None),),
        out_specs=(P("band", "fft", None, None), P(None, "fft", None, None)),
        check_vma=False,
    )
```

```python
import functools
import math

import jax
import jax.numpy as jnp
import ml_dtypes
import numpy as np
from jax import lax
from jax.experimental import pallas as pl
from jax.experimental.pallas import tpu as pltpu
from jax.sharding import PartitionSpec as P

N = 128
SPACING = 0.29
OMEGA = 0.106
MIX = -0.25
VMEM = 32 * 1024 * 1024
SLAB = 8
PLANES = 4
ORBS = 4
SENT = 4
GROUP = 32
LOCAL = N // GROUP
ROWS = ORBS * PLANES
PLACES = [(4 * y_lo + x, 2 * z + y_hi) for y_hi in range(2) for y_lo in range(2) for x in range(4) for z in range(2)]


def split(full):
    high = full.astype(ml_dtypes.bfloat16)
    low = (full - high.astype(np.float64)).astype(ml_dtypes.bfloat16)
    return np.concatenate([high, low], -1)


def cas_tables():
    idx = np.arange(N)
    angle = 2.0 * np.pi / N * (idx[:, None] * idx[None, :] % N)
    full = np.cos(angle) + np.sin(angle)
    to_z = np.zeros((2, 2 * N, 2, N))
    for c in range(2):
        held = [
            (j, (2 * chip + (c ^ q)) * SLAB + 2 * k + p)
            for chip, k in PLACES for j in range(2) for q in range(2) for p in range(2)
        ]
        for row, (j, z) in enumerate(held):
            to_z[c, row, j] = full[z]
    to_z = to_z.reshape(2, 2 * N, 2 * N)
    pairs = [np.stack(np.split(split(t), 2, -1), 1) for t in (to_z, to_z.transpose(0, 2, 1))]
    return [np.concatenate([split(full)] * 2, 0)] + pairs


def halves(value):
    high = value.astype(jnp.bfloat16)
    low = (value - high.astype(jnp.float32)).astype(jnp.bfloat16)
    return high, low


def dot(a, b):
    return lax.dot_general(a, b, (((1,), (0,)), ((), ())), preferred_element_type=jnp.float32)


def rows_by_table(value, right):
    out = dot(jnp.concatenate(halves(value), 1), right)
    return out[:, :N] + out[:, N:]


def turned(value):
    return jnp.concatenate([value[r:r + N].T for r in range(0, value.shape[0], N)], 0)


def spread_kernel(phi_ref, phi_beside_ref, orb_ref, orb_beside_ref, table_ref, out_ref):
    @pl.loop(0, SENT)
    def _(i):
        fields = []
        for j in range(ORBS):
            density = [phi_ref[i, p] * orb_ref[j, p] for p in range(2)]
            density += [phi_beside_ref[i, p] * orb_beside_ref[j, p] for p in range(2)]
            field = turned(rows_by_table(jnp.concatenate(density, 0), table_ref[...]))
            fields.append(rows_by_table(field, table_ref[...]).reshape(PLANES, N, N))
        for j in range(0, ORBS, 2):
            pair = jnp.swapaxes(jnp.concatenate(fields[j:j + 2], 0), 0, 1)
            out_ref[:, i, :, j // 2] = pair.reshape(GROUP, LOCAL, 2 * PLANES, N)


def dot3(value, high, low):
    first, second = halves(value)
    return dot(first, high) + dot(second, high) + dot(first, low)


def line_kernel(in_ref, green_ref, to_z_ref, from_z_ref, out_ref):
    @pl.loop(0, SENT)
    def _(i):
        for a in range(LOCAL):
            green = jnp.concatenate([green_ref[a]] * 2, 1)
            for j in range(ORBS // 2):
                field = in_ref[:, i, a, j].reshape(2 * N, N)
                field = jnp.concatenate([field[:N].T, field[N:].T], 1)
                field = dot3(field, to_z_ref[0], to_z_ref[1]) * green
                field = dot3(field, from_z_ref[0], from_z_ref[1])
                field = jnp.concatenate([field[:, :N].T, field[:, N:].T], 0)
                out_ref[:, i, a, j] = field.reshape(GROUP, 2 * PLANES, N)


def gather_kernel(in_ref, *refs):
    phi_refs, orb_refs, table_ref, applied_refs, owner_refs = refs[:2], refs[2:4], refs[4], refs[5:7], refs[7:]
    for ref in applied_refs:
        ref[...] = jnp.zeros_like(ref)

    @pl.loop(0, SENT)
    def _(i):
        owners = [None, None]
        for pair in range(ORBS // 2):
            both = jnp.swapaxes(in_ref[:, i, :, pair].reshape(N, 2 * PLANES, N), 0, 1)
            for j in (2 * pair, 2 * pair + 1):
                field = both[(j % 2) * PLANES:(j % 2 + 1) * PLANES].reshape(PLANES * N, N)
                field = turned(rows_by_table(field, table_ref[...]))
                result = rows_by_table(field, table_ref[...]).reshape(2, 2, N, N)
                for q in range(2):
                    applied_refs[q][j] += result[q] * phi_refs[q][i]
                    part = result[q] * orb_refs[q][j]
                    owners[q] = part if j == 0 else owners[q] + part
        for ref, owner in zip(owner_refs, owners):
            ref[i] = owner


def join_kernel(in_ref, applied_ref, terms_ref, sems):
    refs = [applied_ref.at[i] for i in range(2)] + [terms_ref.at[i] for i in range(SENT)]
    pairs = [(in_ref.at[k, i], ref.at[pl.ds(2 * k, 2)]) for k in range(4) for i, ref in enumerate(refs)]
    copies = [pltpu.make_async_copy(source, target, sems.at[n]) for n, (source, target) in enumerate(pairs)]
    for copy in copies:
        copy.start()
    for copy in copies:
        copy.wait()


def params():
    return pltpu.CompilerParams(vmem_limit_bytes=VMEM)


def cost(planes):
    return pl.CostEstimate(flops=planes * N * N * 2048, bytes_accessed=planes * N * N * 12, transcendentals=0)


FIELD_SHAPE = jax.ShapeDtypeStruct((GROUP, SENT, LOCAL, ORBS // 2, 2 * PLANES, N), jnp.float32)
PLANE_SHAPE = jax.ShapeDtypeStruct((4, 2, N, N), jnp.float32)


def spread(phis, orbs, table):
    return pl.pallas_call(
        spread_kernel,
        out_shape=FIELD_SHAPE,
        compiler_params=params(),
        cost_estimate=cost(SENT * ROWS),
    )(*phis, *orbs, table)


def lines(field, green, to_z, from_z):
    return pl.pallas_call(
        line_kernel,
        out_shape=FIELD_SHAPE,
        compiler_params=params(),
        cost_estimate=cost(SENT * ROWS),
    )(field, green, to_z, from_z)


def collect(field, phis, orbs, table):
    return pl.pallas_call(
        gather_kernel,
        out_shape=(PLANE_SHAPE,) * 4,
        compiler_params=params(),
        cost_estimate=cost(SENT * ROWS),
    )(field, *phis, *orbs, table)


def join(both):
    return pl.pallas_call(
        join_kernel,
        out_shape=tuple(jax.ShapeDtypeStruct((n, SLAB, N, N), jnp.float32) for n in (2, SENT)),
        in_specs=[pl.BlockSpec(memory_space=pltpu.VMEM)],
        out_specs=(pl.BlockSpec(memory_space=pl.ANY),) * 2,
        scratch_shapes=[pltpu.SemaphoreType.DMA((24,))],
        compiler_params=params(),
    )(both)


def wavenumber(idx):
    shifted = jnp.where(idx < N // 2, idx, idx - N)
    return 2.0 * math.pi / (N * SPACING) * shifted.astype(jnp.float32)


def green_table(group):
    every = jnp.arange(N, dtype=jnp.int32)
    g_y = wavenumber(group * LOCAL + jnp.arange(LOCAL, dtype=jnp.int32))[:, None, None]
    g_z = wavenumber(every)[None, :, None]
    g_x = wavenumber(every)[None, None, :]
    ratio = (g_z * g_z + g_y * g_y + g_x * g_x) / (4.0 * OMEGA * OMEGA)
    safe = jnp.where(ratio > 0, ratio, 1.0)
    kernel = math.pi / (OMEGA * OMEGA) * jnp.where(ratio > 0, -jnp.expm1(-safe) / safe, 1.0)
    return kernel * (MIX / N**3)


def over_core(array):
    return lax.ppermute(array, "fft", [(i, i ^ 1) for i in range(16)])


EVERY = ("band", "fft")
POOLS = [[4 * pool + k for k in range(4)] for pool in range(4)]
LINES = [[(4 * pool + k) * 16 + 2 * chip + c for chip, k in PLACES] for pool in range(4) for c in range(2)]


def swap(array, axis, groups):
    return lax.all_to_all(array, axis, 0, 0, axis_index_groups=groups)


def to_pools(array, moves):
    return lax.ppermute(array, "band", [(4 * a + k, 4 * b + k) for a, b in moves for k in range(4)])


def around(array, distance):
    return to_pools(array, [(p, (p + distance) % 4) for p in range(4)])


def per_device(orbitals):
    place, band = lax.axis_index("fft"), lax.axis_index("band")
    core, pool = place % 2, band // 4
    table, to_z, from_z = (jnp.asarray(t) for t in cas_tables())
    to_z, from_z = (lax.dynamic_index_in_dim(t, core, 0, False) for t in (to_z, from_z))
    green = green_table(band % 2 * 16 + place // 2 * 2 + band // 2 % 2)

    held = swap(jnp.swapaxes(orbitals.reshape(2, 4, 2, N, N), 0, 1), "band", POOLS)
    near = held[0]
    across = to_pools(near, [(0, 2), (2, 0)])
    above = to_pools(near, [(0, 1), (2, 3)])
    below = to_pools(near, [(0, 3), (2, 1)])
    own = jnp.where(core == 0, held[:, 0], held[:, 1])
    orbs = (own, over_core(jnp.where(core == 0, held[:, 1], held[:, 0])))

    def pick(*options):
        return lax.select_n(pool, *options)

    phi = jnp.concatenate([pick(near, above, across, below), pick(across, below, near, above)])
    phis = (phi, over_core(phi))

    phis, orbs, green, to_z, from_z = lax.optimization_barrier((phis, orbs, green, to_z, from_z))
    field = swap(spread(phis, orbs, table), EVERY, LINES)
    field = swap(lines(field, green, to_z, from_z), EVERY, LINES)
    applied, applied_beside, owner, owner_beside = collect(field, phis, orbs, table)

    owner = owner + over_core(owner_beside)

    def part(distance):
        return lax.dynamic_index_in_dim(owner, lax.rem(pool + distance, 4), 0, False)

    share = part(0) + sum(around(part(d), d) for d in (1, 3, 2))
    shares = [share] + [around(share, d) for d in (1, 2, 3)]
    terms = jnp.stack([lax.select_n(pool, *(shares[(p - i) % 4] for p in range(4))) for i in range(SENT)])
    beside = over_core(applied_beside)
    back = jnp.stack([jnp.where(core == 0, applied, beside), jnp.where(core == 0, beside, applied)], 1)
    both = jnp.concatenate([back, jnp.broadcast_to(terms[None], (4,) + terms.shape)], 1)
    return join(swap(both, "band", POOLS))


def solution(mesh):
    return jax.shard_map(
        per_device,
        mesh=mesh,
        in_specs=(P("band", "fft", None, None),),
        out_specs=(P("band", "fft", None, None), P(None, "fft", None, None)),
        check_vma=False,
    )
```
